32 devices in a mesh: len: 8 (over y, x, core), wid: 4 (over z).
Axes of the slice: x: 2, y: 2, z: 4, core: 2. Of those that a mesh axis runs over, the one named last changes fastest.
Arguments:
- ckpt_e: float32 [3, 128, 64, 128], P(None, 'len', 'wid'), may hold values from -6 to 6
- ckpt_h: float32 [3, 128, 64, 128], P(None, 'len', 'wid'), may hold values from -6 to 6
- adj_e: float32 [3, 128, 64, 128], P(None, 'len', 'wid'), may hold values from -6 to 6
- adj_h: float32 [3, 128, 64, 128], P(None, 'len', 'wid'), may hold values from -6 to 6
- material: int32 [128, 64, 128], P('len', 'wid'), may hold values from 0 to 3
- inv_perm: float32 [4], replicated, may hold values from 0.2 to 1
- poling: int32 [16, 8], P('len', 'wid'), may hold values from 0 to 1
- freqs: float32 [8], replicated, may hold values from 0.1 to 3
Outputs:
- adjoint_e: float32 [3, 128, 64, 128], P(None, 'len', 'wid')
- adjoint_h: float32 [3, 128, 64, 128], P(None, 'len', 'wid')
- gradient: float32 [2, 8, 16, 8], P(None, None, 'len', 'wid')
The draws below stay inside these ranges and needn't reach their ends.
All inputs are finite; a program needn't handle non-finite values.
Results may differ from the reference program's by a relative error of at most 0.0001.
Values sent between devices are 32-bit elements; how exact they have to be, the bound alone decides.
A program may use at most 64 MiB of HBM per device.

```python
import math
import jax
import jax.numpy as jnp
from jax import lax

NZ = 128
STEPS = 8
BINS = 8
NMAT = 4
DOMLEN = 8
WBLK = 8
NX = 128
NY = 64
NDOM = 16
NWB = 8


def touch_ends(drawn, stream_key, least, high):
    shape = drawn.shape
    index_at = [jax.random.randint(jax.random.fold_in(stream_key, axis), (), 0, shape[axis]) for axis in range(len(shape))]
    drawn = drawn.at[tuple(index_at)].set(least)
    longest = shape.index(max(shape))
    index_at[longest] = (index_at[longest] + 1) % shape[longest]
    return drawn.at[tuple(index_at)].set(high)


def block_scale(stream_key, extent, shards, smallest, high):
    level = 1.0
    for position, shards_of in shards:
        draws = jax.random.uniform(jax.random.fold_in(jax.random.fold_in(stream_key, 6), position), (shards_of,), jnp.float32, smallest / len(shards), high / len(shards))
        level = level * jnp.repeat(jnp.exp(draws), extent[position] // shards_of).reshape((-1,) + (1,) * (len(extent) - 1 - position))
    return level


def centred(stream_key, dims, deviation, most, cuts=(), kind=jnp.bfloat16):
    loudness = block_scale(stream_key, dims, cuts, -0.22, 0.18) if cuts else 1.0
    array = jax.random.normal(stream_key, dims, jnp.float32) * deviation * loudness
    return jnp.minimum(jnp.maximum(array, -most), most).astype(kind)


def setup_inputs(seed: int = 0) -> dict:
    splits = jax.random.split(jax.random.key(seed), 9)
    ckpt_e = centred(splits[0], (3, NX, NY, NZ), 1.0, 6.0, ((1, 8), (2, 4)), jnp.float32)
    ckpt_h = centred(splits[1], (3, NX, NY, NZ), 1.0, 6.0, ((1, 8), (2, 4)), jnp.float32)
    adj_e = centred(splits[2], (3, NX, NY, NZ), 1.0, 6.0, ((1, 8), (2, 4)), jnp.float32)
    adj_h = centred(splits[3], (3, NX, NY, NZ), 1.0, 6.0, ((1, 8), (2, 4)), jnp.float32)
    material = touch_ends(jax.random.randint(splits[4], (NX, NY, NZ), 0, NMAT), jax.random.fold_in(splits[4], 1), 0, NMAT - 1).astype(jnp.int32)
    inv_perm = jnp.clip(jax.random.uniform(splits[5], (NMAT,), jnp.float32, 0.2, 1.0), 0.2, 1.0)
    poling = touch_ends(jax.random.randint(splits[6], (NDOM, NWB), 0, 2), jax.random.fold_in(splits[6], 1), 0, 1).astype(jnp.int32)
    freqs = jnp.clip(jax.random.uniform(splits[7], (BINS,), jnp.float32, 0.1, 3.0), 0.1, 3.0)
    return {"ckpt_e": ckpt_e, "ckpt_h": ckpt_h, "adj_e": adj_e, "adj_h": adj_h, "material": material, "inv_perm": inv_perm, "poling": poling, "freqs": freqs}


COURANT = 0.5
OMEGA = 0.9

def forward_diff(field, axis):
    widths = [(0, 0), (0, 0), (0, 0)]
    widths[axis] = (0, 1)
    padded = jnp.pad(field, widths)
    return lax.slice_in_dim(padded, 1, field.shape[axis] + 1, axis=axis) - field

def backward_diff(field, axis):
    widths = [(0, 0), (0, 0), (0, 0)]
    widths[axis] = (1, 0)
    padded = jnp.pad(field, widths)
    return field - lax.slice_in_dim(padded, 0, field.shape[axis], axis=axis)

def curl_electric(electric):
    comp_x, comp_y, comp_z = (electric[0], electric[1], electric[2])
    return jnp.stack([forward_diff(comp_z, 1) - forward_diff(comp_y, 2), forward_diff(comp_x, 2) - forward_diff(comp_z, 0), forward_diff(comp_y, 0) - forward_diff(comp_x, 1)])

def curl_magnetic(magnetic):
    comp_x, comp_y, comp_z = (magnetic[0], magnetic[1], magnetic[2])
    return jnp.stack([backward_diff(comp_z, 1) - backward_diff(comp_y, 2), backward_diff(comp_x, 2) - backward_diff(comp_z, 0), backward_diff(comp_y, 0) - backward_diff(comp_x, 1)])

def reference(ckpt_e, ckpt_h, adj_e, adj_h, material, inv_perm, poling, freqs):
    inv_eps = jnp.zeros(material.shape, jnp.float32)
    for index in range(NMAT):
        inv_eps = inv_eps + (material == index).astype(jnp.float32) * inv_perm[index]
    chi = (material == 0).astype(jnp.float32)
    signs = (2 * poling - 1).astype(jnp.float32)
    sign_full = jnp.repeat(jnp.repeat(signs, DOMLEN, axis=0), WBLK, axis=1)
    phase = math.pi / DOMLEN * jnp.arange(NX).astype(jnp.float32)
    terms = jnp.stack([sign_full * jnp.cos(phase)[:, None], sign_full * jnp.sin(phase)[:, None]])
    envelope = jnp.cumsum(terms, axis=1) / math.sqrt(NX)
    electric, magnetic = (ckpt_e, ckpt_h)
    stored = []
    for moment in range(STEPS):
        magnetic = magnetic - COURANT * curl_electric(electric)
        electric = electric + COURANT * inv_eps * curl_magnetic(magnetic)
        stored.append(electric)
    adjoint_e, adjoint_h = (adj_e, adj_h)
    gradient = jnp.zeros((2, BINS, NDOM, NWB), jnp.float32)
    scale = 1.0 / math.sqrt(DOMLEN * WBLK * NZ)
    for moment in range(STEPS, 0, -1):
        forward_field = stored[moment - 1]
        drive = envelope[0] * math.cos(OMEGA * moment) + envelope[1] * math.sin(OMEGA * moment)
        adjoint_e = adjoint_e + drive[None, :, :, None] * chi * forward_field
        product = chi * lax.optimization_barrier(jnp.sum(adjoint_e * forward_field, axis=0))
        blocks = product.reshape(NDOM, DOMLEN, NWB, WBLK, NZ).sum(axis=(1, 3, 4)) * scale
        angles = freqs * moment
        gradient = gradient + jnp.stack([jnp.cos(angles)[:, None, None] * blocks, -jnp.sin(angles)[:, None, None] * blocks])
        adjoint_e = adjoint_e - COURANT * inv_eps * curl_magnetic(adjoint_h)
        adjoint_h = adjoint_h + COURANT * curl_electric(adjoint_e)
    return (adjoint_e, adjoint_h, gradient)
```

```python
import math

import jax
import jax.numpy as jnp
from jax import lax
from jax.experimental import pallas as pl
from jax.experimental.pallas import tpu as pltpu
from jax.sharding import PartitionSpec as P

STEPS = 8
DOMLEN = 8
WBLK = 8
COURANT = 0.5
OMEGA = 0.9
MESH = pl.DeviceIdType.MESH
LO = 8
VERSIONS = 2 * STEPS + 1


def zforward(value, lane):
    depth = value.shape[-1]
    return jnp.where(lane < depth - 1, pltpu.roll(value, depth - 1, 1), 0.0)


def zbackward(value, lane):
    return jnp.where(lane > 0, pltpu.roll(value, 1, 1), 0.0)


def make_kernel(count, wcount, nx, ny, nz, bins, nmat):
    top = LO + ny
    dom_len, dom_wid = nx // DOMLEN, ny // WBLK
    span = count * nx

    def kernel(
        ckpt_e, ckpt_h, adj_e, adj_h, material, inv_perm, poling, freqs,
        out_e, out_h, out_g,
        fields, mags, coef, envc, prods, pre, pre_out,
        ysend_hi, ysend_lo, yrecv_lo, yrecv_hi, hsend, hrecv,
        send_sem, recv_sem, hsend_sem, hrecv_sem, psend_sem, precv_sem,
    ):
        me, row = lax.axis_index("len"), lax.axis_index("wid")
        has_prev, has_next = me > 0, me < count - 1
        has_low, has_high = row > 0, row < wcount - 1
        own = pl.ds(LO, ny)

        for v in range(VERSIONS):
            if v == STEPS:
                continue
            for c in range(3):
                fields[v, c, 0, own] = jnp.zeros((ny, nz), jnp.float32)
                fields[v, c, nx + 1, own] = jnp.zeros((ny, nz), jnp.float32)
            fields[v, 0, 0, pl.ds(top, 8)] = jnp.zeros((8, nz), jnp.float32)
            fields[v, 1, nx + 1, pl.ds(0, LO)] = jnp.zeros((LO, nz), jnp.float32)
            yrecv_lo[v] = jnp.zeros((3, nx, nz), jnp.float32)
            yrecv_hi[v] = jnp.zeros((2, nx, nz), jnp.float32)
        hrecv[...] = jnp.zeros(hrecv.shape, jnp.float32)
        pre[...] = jnp.zeros(pre.shape, jnp.float32)
        for h in range(2):
            for c in range(3):
                mags[h, c, 0] = jnp.zeros((top, nz), jnp.float32)

        barrier = pltpu.get_barrier_semaphore()

        def greet(there, len_to, wid_to):
            @pl.when(there)
            def _():
                pl.semaphore_signal(
                    barrier, inc=1, device_id={"len": len_to, "wid": wid_to}, device_id_type=MESH
                )

        for off in range(1, count):
            greet(me + off < count, me + off, row)
            greet(me - off >= 0, me - off, row)
        greet(has_low, me, row - 1)
        greet(has_high, me, row + 1)
        greet(has_next & has_low, me + 1, row - 1)
        greet(has_prev & has_high, me - 1, row + 1)

        for x in range(nx):
            for c in range(3):
                fields[0, c, x + 1, own] = ckpt_e[c, x]
                mags[0, c, x + 1, own] = ckpt_h[c, x]
                mags[1, c, x + 1, own] = adj_h[c, x]
                ysend_hi[0, c, pl.ds(x, 1)] = ckpt_e[c, x, pl.ds(ny - 1, 1)]
            for slot, c in enumerate((0, 2)):
                ysend_lo[0, slot, pl.ds(x, 1)] = ckpt_e[c, x, pl.ds(0, 1)]
                hsend[0, slot, pl.ds(x, 1)] = ckpt_h[c, x, pl.ds(ny - 1, 1)]
                hsend[1, slot, pl.ds(x, 1)] = adj_h[c, x, pl.ds(ny - 1, 1)]

        rows = lax.broadcasted_iota(jnp.int32, (ny, nz), 0)
        signs = []
        for d in range(dom_len):
            sign = jnp.zeros((ny, nz), jnp.float32)
            for w in range(dom_wid):
                value = (2 * poling[d, w] - 1).astype(jnp.float32)
                sign = jnp.where(rows // WBLK == w, value, sign)
            signs.append(sign)
        parity = jnp.float32(1.0)
        if dom_len % 2:
            parity = (1 - 2 * (me % 2)).astype(jnp.float32)
        waves = [
            [f(math.pi * x / DOMLEN) / math.sqrt(span) for x in range(nx)] for f in (math.cos, math.sin)
        ]
        for c in range(2):
            total = jnp.zeros((ny, nz), jnp.float32)
            for d in range(dom_len):
                total = total + signs[d] * sum(waves[c][d * DOMLEN : (d + 1) * DOMLEN])
            pre_out[c] = total * parity

        greeted = (
            (count - 1)
            + has_low.astype(jnp.int32)
            + has_high.astype(jnp.int32)
            + (has_next & has_low).astype(jnp.int32)
            + (has_prev & has_high).astype(jnp.int32)
        )
        pl.semaphore_wait(barrier, greeted)

        def remote(src, dst, send, recv, len_to, wid_to):
            return pltpu.make_async_remote_copy(
                src_ref=src, dst_ref=dst, send_sem=send, recv_sem=recv,
                device_id={"len": len_to, "wid": wid_to}, device_id_type=MESH,
            )

        def halo(v):
            f = fields.at[v]
            pairs = (
                (has_next, has_prev, f.at[:, nx, own], f.at[:, 0, own], me + 1, row),
                (has_prev, has_next, f.at[pl.ds(1, 2), 1, own], f.at[pl.ds(1, 2), nx + 1, own], me - 1, row),
                (has_high, has_low, ysend_hi.at[v], yrecv_lo.at[v], me, row + 1),
                (has_low, has_high, ysend_lo.at[v], yrecv_hi.at[v], me, row - 1),
                (has_next & has_low, has_prev & has_high,
                 f.at[0, nx, pl.ds(LO, 8)], f.at[0, 0, pl.ds(top, 8)], me + 1, row - 1),
                (has_prev & has_high, has_next & has_low,
                 f.at[1, 1, pl.ds(top - 8, 8)], f.at[1, nx + 1, pl.ds(0, LO)], me - 1, row + 1),
            )
            return [
                (sends, gets, remote(src, dst, send_sem.at[v, i], recv_sem.at[v, i], lt, wt))
                for i, (sends, gets, src, dst, lt, wt) in enumerate(pairs)
            ]

        def first_halo():
            pairs = (
                (has_next, has_prev, ckpt_h.at[pl.ds(1, 2), nx - 1], mags.at[0, pl.ds(1, 2), 0, own], me + 1, row),
                (has_next, has_prev, adj_h.at[pl.ds(1, 2), nx - 1], mags.at[1, pl.ds(1, 2), 0, own], me + 1, row),
                (has_high, has_low, hsend, hrecv, me, row + 1),
            )
            return [
                (sends, gets, remote(src, dst, hsend_sem.at[i], hrecv_sem.at[i], lt, wt))
                for i, (sends, gets, src, dst, lt, wt) in enumerate(pairs)
            ]

        def prefix_copies():
            return [
                (me + off < count, me - off >= 0,
                 remote(pre_out, pre.at[off], psend_sem.at[off], precv_sem.at[off], me + off, row))
                for off in range(1, count)
            ]

        def start(copies):
            for sends, _, copy in copies:
                pl.when(sends)(copy.start)

        def arrive(copies):
            for _, gets, copy in copies:
                pl.when(gets)(copy.wait_recv)

        def leave(copies):
            for sends, _, copy in copies:
                pl.when(sends)(copy.wait_send)

        start(halo(0))
        start(first_halo())
        start(prefix_copies())

        for x in range(nx):
            value = jnp.zeros((ny, nz), jnp.float32)
            for index in range(nmat):
                value = jnp.where(material[x] == index, COURANT * inv_perm[index], value)
            coef[x] = value
        bin_row = lax.broadcasted_iota(jnp.int32, (bins, nz), 0)
        bin_lane = lax.broadcasted_iota(jnp.int32, (bins, nz), 1)
        bin_freq = jnp.zeros((bins, nz), jnp.float32)
        for k in range(bins):
            bin_freq = jnp.where(bin_row == k, freqs[k], bin_freq)
        angles = bin_freq * bin_lane.astype(jnp.float32)
        cosines, sines = jnp.cos(angles), jnp.sin(angles)
        out_g[...] = jnp.zeros(out_g.shape, jnp.float32)

        lane_h = lax.broadcasted_iota(jnp.int32, (top, nz), 1)
        row_h = lax.broadcasted_iota(jnp.int32, (top, nz), 0)
        lane = lax.broadcasted_iota(jnp.int32, (ny, nz), 1)
        half = jnp.where((row_h >= LO) | has_low, COURANT, 0.0)
        whole = pl.ds(0, top)
        above = pl.ds(1, top)
        below = pl.ds(LO - 1, ny)

        def update_h(h, v, factor):
            def unpack(x, carry):
                for c in range(3):
                    fields[v, c, x + 1, pl.ds(LO - 1, 1)] = yrecv_lo[v, c, pl.ds(x, 1)]
                for slot, c in enumerate((0, 2)):
                    fields[v, c, x + 1, pl.ds(top, 1)] = yrecv_hi[v, slot, pl.ds(x, 1)]
                return carry

            lax.fori_loop(0, nx, unpack, 0, unroll=4)

            def column(x):
                ex, ey, ez = (fields[v, c, x, whole] for c in range(3))
                ex_y, ez_y = fields[v, 0, x, above], fields[v, 2, x, above]
                ey_x, ez_x = fields[v, 1, x + 1, whole], fields[v, 2, x + 1, whole]
                curl_x = (ez_y - ez) - (zforward(ey, lane_h) - ey)
                curl_y = (zforward(ex, lane_h) - ex) - (ez_x - ez)
                curl_z = (ey_x - ey) - (ex_y - ex)
                mags[h, 0, x] = mags[h, 0, x] + factor * curl_x
                mags[h, 1, x] = mags[h, 1, x] + factor * curl_y
                mags[h, 2, x] = mags[h, 2, x] + factor * curl_z

            @pl.when(has_prev)
            def _():
                column(0)

            def body(x, carry):
                column(x)
                return carry

            lax.fori_loop(1, nx + 1, body, 0, unroll=2)

        def curl_h(h, x):
            hx, hy, hz = (mags[h, c, x, own] for c in range(3))
            hx_y, hz_y = mags[h, 0, x, below], mags[h, 2, x, below]
            hy_x, hz_x = mags[h, 1, x - 1, own], mags[h, 2, x - 1, own]
            return (
                (hz - hz_y) - (hy - zbackward(hy, lane)),
                (hx - zbackward(hx, lane)) - (hz - hz_x),
                (hy - hy_x) - (hx - hx_y),
            )

        def put(v, x, values):
            for c in range(3):
                fields[v, c, x, own] = values[c]
                ysend_hi[v, c, pl.ds(x - 1, 1)] = values[c][ny - 1 :]
            for slot, c in enumerate((0, 2)):
                ysend_lo[v, slot, pl.ds(x - 1, 1)] = values[c][:1]

        def update_e(v):
            def body(x, carry):
                curls = curl_h(0, x)
                scale = coef[x - 1]
                put(v + 1, x, [fields[v, c, x, own] + scale * curls[c] for c in range(3)])
                return carry

            lax.fori_loop(1, nx + 1, body, 0, unroll=2)

        def update_adjoint(n, held, v, turn_cos, turn_sin):
            for d in range(dom_len):

                def body(x, total):
                    now = [fields[n, c, x, own] for c in range(3)]
                    drive = envc[0, x - 1] * turn_cos + envc[1, x - 1] * turn_sin
                    driven = [held(c, x) + drive * now[c] for c in range(3)]
                    dot = driven[0] * now[0] + driven[1] * now[1] + driven[2] * now[2]
                    total = total + jnp.where(material[x - 1] == 0, dot, 0.0)
                    curls = curl_h(1, x)
                    scale = coef[x - 1]
                    put(v, x, [driven[c] - scale * curls[c] for c in range(3)])
                    return total

                prods[d] = lax.fori_loop(
                    1 + d * DOMLEN, 1 + (d + 1) * DOMLEN, body, jnp.zeros((ny, nz), jnp.float32), unroll=2
                )

        def add_gradient(n):
            norm = 1.0 / math.sqrt(DOMLEN * WBLK * nz)
            sums = jnp.zeros((1, nz), jnp.float32)
            lane_g = lax.broadcasted_iota(jnp.int32, (1, nz), 1)
            for d in range(dom_len):
                for w in range(dom_wid):
                    block = prods[d, pl.ds(w * WBLK, WBLK)]
                    partial = jnp.sum(jnp.sum(block, axis=0, keepdims=True), axis=1, keepdims=True)
                    sums = jnp.where(lane_g == d * dom_wid + w, partial * norm, sums)
            cos_n = jnp.sum(jnp.where(bin_lane == n, cosines, 0.0), axis=1, keepdims=True)
            sin_n = jnp.sum(jnp.where(bin_lane == n, sines, 0.0), axis=1, keepdims=True)
            out_g[pl.ds(0, bins)] = out_g[pl.ds(0, bins)] + cos_n * sums
            out_g[pl.ds(bins, bins)] = out_g[pl.ds(bins, bins)] - sin_n * sums

        arrive(first_halo())
        for h in range(2):
            for slot, c in enumerate((0, 2)):
                for x in range(nx):
                    mags[h, c, x + 1, pl.ds(LO - 1, 1)] = hrecv[h, slot, pl.ds(x, 1)]

        def forward(v, carry):
            arrive(halo(v))
            update_h(0, v, -half)
            update_e(v)

            @pl.when(v < STEPS - 1)
            def _():
                start(halo(v + 1))

            return carry

        lax.fori_loop(0, STEPS, forward, 0)

        arrive(prefix_copies())
        for c in range(2):
            running = jnp.zeros((ny, nz), jnp.float32)
            for off in range(count - 1, 0, -1):
                running = running + pre[off, c]
            for x in range(nx):
                running = running + signs[x // DOMLEN] * (parity * waves[c][x])
                envc[c, x] = jnp.where(material[x] == 0, running, 0.0)

        update_adjoint(
            STEPS, lambda c, x: adj_e[c, x - 1], STEPS + 1, math.cos(OMEGA * STEPS), math.sin(OMEGA * STEPS)
        )

        def backward(m, carry):
            v = STEPS + 1 + m
            n = STEPS - 1 - m
            start(halo(v))
            add_gradient(n + 1)
            turn_cos = turn_sin = jnp.float32(0.0)
            for moment in range(1, STEPS):
                turn_cos = jnp.where(n == moment, math.cos(OMEGA * moment), turn_cos)
                turn_sin = jnp.where(n == moment, math.sin(OMEGA * moment), turn_sin)
            arrive(halo(v))
            update_h(1, v, half)
            update_adjoint(n, lambda c, x: fields[v, c, x, own], v + 1, turn_cos, turn_sin)
            return carry

        lax.fori_loop(0, STEPS - 1, backward, 0)

        last = VERSIONS - 1
        start(halo(last))
        add_gradient(1)
        for x in range(nx):
            for c in range(3):
                out_e[c, x] = fields[last, c, x + 1, own]
        arrive(halo(last))
        update_h(1, last, half)
        for x in range(nx):
            for c in range(3):
                out_h[c, x] = mags[1, c, x + 1, own]

        leave(first_halo())
        leave(prefix_copies())

        def drain(v, carry):
            @pl.when(v != STEPS)
            def _():
                leave(halo(v))

            return carry

        lax.fori_loop(0, VERSIONS, drain, 0)

    f32 = jnp.float32
    vmem = pl.BlockSpec(memory_space=pltpu.VMEM)
    smem = pl.BlockSpec(memory_space=pltpu.SMEM)
    return pl.pallas_call(
        kernel,
        out_shape=(
            jax.ShapeDtypeStruct((3, nx, ny, nz), f32),
            jax.ShapeDtypeStruct((3, nx, ny, nz), f32),
            jax.ShapeDtypeStruct((2 * bins, nz), f32),
        ),
        in_specs=[vmem, vmem, vmem, vmem, vmem, smem, smem, smem],
        out_specs=(vmem, vmem, vmem),
        scratch_shapes=[
            pltpu.VMEM((VERSIONS, 3, nx + 2, top + 8, nz), f32),
            pltpu.VMEM((2, 3, nx + 1, top, nz), f32),
            pltpu.VMEM((nx, ny, nz), f32),
            pltpu.VMEM((2, nx, ny, nz), f32),
            pltpu.VMEM((dom_len, ny, nz), f32),
            pltpu.VMEM((count, 2, ny, nz), f32),
            pltpu.VMEM((2, ny, nz), f32),
            pltpu.VMEM((VERSIONS, 3, nx, nz), f32),
            pltpu.VMEM((VERSIONS, 2, nx, nz), f32),
            pltpu.VMEM((VERSIONS, 3, nx, nz), f32),
            pltpu.VMEM((VERSIONS, 2, nx, nz), f32),
            pltpu.VMEM((2, 2, nx, nz), f32),
            pltpu.VMEM((2, 2, nx, nz), f32),
            pltpu.SemaphoreType.DMA((VERSIONS, 6)),
            pltpu.SemaphoreType.DMA((VERSIONS, 6)),
            pltpu.SemaphoreType.DMA((3,)),
            pltpu.SemaphoreType.DMA((3,)),
            pltpu.SemaphoreType.DMA((count,)),
            pltpu.SemaphoreType.DMA((count,)),
        ],
        compiler_params=pltpu.CompilerParams(
            collective_id=0, has_side_effects=True, vmem_limit_bytes=48 * 1024 * 1024
        ),
    )


def solution(mesh):
    count, wcount = mesh.shape["len"], mesh.shape["wid"]

    def per_device(ckpt_e, ckpt_h, adj_e, adj_h, material, inv_perm, poling, freqs):
        nx, ny, nz = material.shape
        bins = freqs.shape[0]
        call = make_kernel(count, wcount, nx, ny, nz, bins, inv_perm.shape[0])
        adjoint_e, adjoint_h, grad = call(
            ckpt_e, ckpt_h, adj_e, adj_h, material, inv_perm, poling, freqs
        )
        dom_len, dom_wid = nx // DOMLEN, ny // WBLK
        gradient = grad[:, : dom_len * dom_wid].reshape(2, bins, dom_len, dom_wid)
        return adjoint_e, adjoint_h, gradient

    field = P(None, "len", "wid", None)
    in_specs = (field, field, field, field, P("len", "wid", None), P(), P("len", "wid"), P())
    out_specs = (field, field, P(None, None, "len", "wid"))
    return jax.shard_map(
        per_device, mesh=mesh, in_specs=in_specs, out_specs=out_specs, check_vma=False
    )
```

```python
import math

import jax
import jax.numpy as jnp
from jax import lax
from jax.experimental import pallas as pl
from jax.experimental.pallas import tpu as pltpu
from jax.sharding import PartitionSpec as P

STEPS = 8
DOMLEN = 8
WBLK = 8
COURANT = 0.5
OMEGA = 0.9
MESH = pl.DeviceIdType.MESH
LO = 8
VERSIONS = 2 * STEPS + 1


def zforward(value, lane):
    depth = value.shape[-1]
    return jnp.where(lane < depth - 1, pltpu.roll(value, depth - 1, 1), 0.0)


def zbackward(value, lane):
    return jnp.where(lane > 0, pltpu.roll(value, 1, 1), 0.0)


def make_kernel(count, wcount, nx, ny, nz, bins, nmat):
    top = LO + ny
    dom_len, dom_wid = nx // DOMLEN, ny // WBLK
    span = count * nx

    def kernel(
        ckpt_e, ckpt_h, adj_e, adj_h, cells, inv_perm, poling, freqs,
        out_e, out_h, out_g,
        fields, mags, material, coef, envc, prods, pre, pre_out,
        ysend_hi, ysend_lo, yrecv_lo, yrecv_hi, hsend, hrecv, ypad,
        load_sem, send_sem, recv_sem, hsend_sem, hrecv_sem, psend_sem, precv_sem,
    ):
        me, row = lax.axis_index("len"), lax.axis_index("wid")
        has_prev, has_next = me > 0, me < count - 1
        has_low, has_high = row > 0, row < wcount - 1
        own = pl.ds(LO, ny)

        loads = [
            pltpu.make_async_copy(src, dst, load_sem.at[i])
            for i, (src, dst) in enumerate((
                (ckpt_e, fields.at[0, :, pl.ds(1, nx), own]),
                (ckpt_h, mags.at[0, :, pl.ds(1, nx), own]),
                (adj_h, mags.at[1, :, pl.ds(1, nx), own]),
                (cells, material),
                (adj_e, fields.at[VERSIONS, :, pl.ds(1, nx), own]),
            ))
        ]
        for load in loads:
            load.start()

        for v in range(VERSIONS):
            if v != STEPS:
                fields[v, 0, 0, pl.ds(top, 8)] = jnp.zeros((8, nz), jnp.float32)
                fields[v, 1, nx + 1, pl.ds(0, LO)] = jnp.zeros((LO, nz), jnp.float32)
        pre[...] = jnp.zeros(pre.shape, jnp.float32)
        for h in range(2):
            for c in range(3):
                mags[h, c, 0] = jnp.zeros((top, nz), jnp.float32)
                for x in range(nx):
                    mags[h, c, x + 1, pl.ds(0, LO)] = jnp.zeros((LO, nz), jnp.float32)

        barrier = pltpu.get_barrier_semaphore()

        def greet(there, len_to, wid_to):
            @pl.when(there)
            def _():
                pl.semaphore_signal(
                    barrier, inc=1, device_id={"len": len_to, "wid": wid_to}, device_id_type=MESH
                )

        for off in range(1, count):
            greet(me + off < count, me + off, row)
            greet(me - off >= 0, me - off, row)
        greet(has_low, me, row - 1)
        greet(has_high, me, row + 1)
        greet(has_next & has_low, me + 1, row - 1)
        greet(has_prev & has_high, me - 1, row + 1)

        rows = lax.broadcasted_iota(jnp.int32, (ny, nz), 0)
        signs = []
        for d in range(dom_len):
            sign = jnp.zeros((ny, nz), jnp.float32)
            for w in range(dom_wid):
                value = (2 * poling[d, w] - 1).astype(jnp.float32)
                sign = jnp.where(rows // WBLK == w, value, sign)
            signs.append(sign)
        parity = jnp.float32(1.0)
        if dom_len % 2:
            parity = (1 - 2 * (me % 2)).astype(jnp.float32)
        waves = [
            [f(math.pi * x / DOMLEN) / math.sqrt(span) for x in range(nx)] for f in (math.cos, math.sin)
        ]
        for c in range(2):
            total = jnp.zeros((ny, nz), jnp.float32)
            for d in range(dom_len):
                total = total + signs[d] * sum(waves[c][d * DOMLEN : (d + 1) * DOMLEN])
            pre_out[c] = total * parity

        greeted = (
            (count - 1)
            + has_low.astype(jnp.int32)
            + has_high.astype(jnp.int32)
            + (has_next & has_low).astype(jnp.int32)
            + (has_prev & has_high).astype(jnp.int32)
        )
        pl.semaphore_wait(barrier, greeted)

        def remote(src, dst, send, recv, len_to, wid_to):
            return pltpu.make_async_remote_copy(
                src_ref=src, dst_ref=dst, send_sem=send, recv_sem=recv,
                device_id={"len": len_to, "wid": wid_to}, device_id_type=MESH,
            )

        def halo(v):
            f = fields.at[v]
            pairs = (
                (has_next, has_prev, f.at[:, nx, own], f.at[:, 0, own], me + 1, row),
                (has_prev, has_next, f.at[pl.ds(1, 2), 1, own], f.at[pl.ds(1, 2), nx + 1, own], me - 1, row),
                (has_high, has_low, ysend_hi.at[v], yrecv_lo.at[v], me, row + 1),
                (has_low, has_high, ysend_lo.at[v], yrecv_hi.at[v], me, row - 1),
                (has_next & has_low, has_prev & has_high,
                 f.at[0, nx, pl.ds(LO, 8)], f.at[0, 0, pl.ds(top, 8)], me + 1, row - 1),
                (has_prev & has_high, has_next & has_low,
                 f.at[1, 1, pl.ds(top - 8, 8)], f.at[1, nx + 1, pl.ds(0, LO)], me - 1, row + 1),
            )
            return [
                (sends, gets, remote(src, dst, send_sem.at[v, i], recv_sem.at[v, i], lt, wt))
                for i, (sends, gets, src, dst, lt, wt) in enumerate(pairs)
            ]

        def first_halo():
            pairs = (
                (has_next, has_prev, ckpt_h.at[pl.ds(1, 2), nx - 1], mags.at[0, pl.ds(1, 2), 0, own], me + 1, row),
                (has_next, has_prev, adj_h.at[pl.ds(1, 2), nx - 1], mags.at[1, pl.ds(1, 2), 0, own], me + 1, row),
                (has_high, has_low, hsend, hrecv, me, row + 1),
            )
            return [
                (sends, gets, remote(src, dst, hsend_sem.at[i], hrecv_sem.at[i], lt, wt))
                for i, (sends, gets, src, dst, lt, wt) in enumerate(pairs)
            ]

        def prefix_copies():
            return [
                (me + off < count, me - off >= 0,
                 remote(pre_out, pre.at[off], psend_sem.at[off], precv_sem.at[off], me + off, row))
                for off in range(1, count)
            ]

        def start(copies):
            for sends, _, copy in copies:
                pl.when(sends)(copy.start)

        def arrive(copies):
            for _, gets, copy in copies:
                pl.when(gets)(copy.wait_recv)

        def leave(copies):
            for sends, _, copy in copies:
                pl.when(sends)(copy.wait_send)

        for load in loads[:3]:
            load.wait()
        for x in range(nx):
            at, end = pl.ds(x, 1), pl.ds(top - 1, 1)
            for c in range(3):
                ysend_hi[0, c, at] = fields[0, c, x + 1, end]
            for slot, c in enumerate((0, 2)):
                ysend_lo[0, slot, at] = fields[0, c, x + 1, pl.ds(LO, 1)]
                hsend[0, slot, at] = mags[0, c, x + 1, end]
                hsend[1, slot, at] = mags[1, c, x + 1, end]
        start(halo(0))
        start(first_halo())
        start(prefix_copies())

        loads[3].wait()
        loads[4].wait()
        for x in range(nx):
            value = jnp.zeros((ny, nz), jnp.float32)
            for index in range(nmat):
                value = jnp.where(material[x] == index, COURANT * inv_perm[index], value)
            coef[x] = value
        bin_row = lax.broadcasted_iota(jnp.int32, (bins, nz), 0)
        bin_lane = lax.broadcasted_iota(jnp.int32, (bins, nz), 1)
        bin_freq = jnp.zeros((bins, nz), jnp.float32)
        for k in range(bins):
            bin_freq = jnp.where(bin_row == k, freqs[k], bin_freq)
        angles = bin_freq * bin_lane.astype(jnp.float32)
        cosines, sines = jnp.cos(angles), jnp.sin(angles)
        out_g[...] = jnp.zeros(out_g.shape, jnp.float32)

        lane = lax.broadcasted_iota(jnp.int32, (ny, nz), 1)
        lane_x = lax.broadcasted_iota(jnp.int32, (nx, nz), 1)
        above = pl.ds(LO + 1, ny)
        below = pl.ds(LO - 1, ny)

        def curl_e(v, x, ey_x, ez_x):
            ex, ey, ez = (fields[v, c, x, own] for c in range(3))
            ex_y = jnp.where(rows < ny - 1, fields[v, 0, x, above], 0.0)
            ez_y = jnp.where(rows < ny - 1, fields[v, 2, x, above], 0.0)
            return (
                (ez_y - ez) - (zforward(ey, lane) - ey),
                (zforward(ex, lane) - ex) - (ez_x - ez),
                (ey_x - ey) - (ex_y - ex),
            )

        def inner_h(h, v, factor):
            def add(x, curls):
                for c in range(3):
                    mags[h, c, x, own] = mags[h, c, x, own] + factor * curls[c]

            def body(x, carry):
                add(x, curl_e(v, x, fields[v, 1, x + 1, own], fields[v, 2, x + 1, own]))
                return carry

            lax.fori_loop(1, nx, body, 0, unroll=nx - 1)
            zero = jnp.zeros((ny, nz), jnp.float32)
            add(nx, curl_e(v, nx, zero, zero))

        def edge_h(h, v, factor):
            @pl.when(has_next)
            def _():
                mags[h, 1, nx, own] = mags[h, 1, nx, own] - factor * fields[v, 2, nx + 1, own]
                mags[h, 2, nx, own] = mags[h, 2, nx, own] + factor * fields[v, 1, nx + 1, own]

            @pl.when(has_high)
            def _():
                end = pl.ds(top - 1, 1)
                for x in range(nx):
                    at = pl.ds(x, 1)
                    mags[h, 0, x + 1, end] = mags[h, 0, x + 1, end] + factor * yrecv_hi[v, 1, at]
                    mags[h, 2, x + 1, end] = mags[h, 2, x + 1, end] - factor * yrecv_hi[v, 0, at]

            @pl.when(has_prev)
            def _():
                ex, ey, ez = (fields[v, c, 0, own] for c in range(3))
                curl_y = (zforward(ex, lane) - ex) - (fields[v, 2, 1, own] - ez)
                curl_z = (fields[v, 1, 1, own] - ey) - (fields[v, 0, 0, above] - ex)
                mags[h, 1, 0, own] = mags[h, 1, 0, own] + factor * curl_y
                mags[h, 2, 0, own] = mags[h, 2, 0, own] + factor * curl_z

            @pl.when(has_low)
            def _():
                ex, ey, ez = (yrecv_lo[v, c] for c in range(3))
                ypad[pl.ds(0, nx)] = ey
                ypad[pl.ds(nx, 1)] = fields[v, 1, nx + 1, pl.ds(LO - 1, 1)]
                ey_x = ypad[pl.ds(1, nx)]
                curl_x = (ysend_lo[v, 1] - ez) - (zforward(ey, lane_x) - ey)
                curl_z = (ey_x - ey) - (ysend_lo[v, 0] - ex)
                hrecv[h, 0] = hrecv[h, 0] + factor * curl_x
                hrecv[h, 1] = hrecv[h, 1] + factor * curl_z
                unpack_h(h)

        def unpack_h(h):
            for slot, c in enumerate((0, 2)):
                for x in range(nx):
                    mags[h, c, x + 1, pl.ds(LO - 1, 1)] = hrecv[h, slot, pl.ds(x, 1)]

        def curl_h(h, x):
            hx, hy, hz = (mags[h, c, x, own] for c in range(3))
            hx_y, hz_y = mags[h, 0, x, below], mags[h, 2, x, below]
            hy_x, hz_x = mags[h, 1, x - 1, own], mags[h, 2, x - 1, own]
            return (
                (hz - hz_y) - (hy - zbackward(hy, lane)),
                (hx - zbackward(hx, lane)) - (hz - hz_x),
                (hy - hy_x) - (hx - hx_y),
            )

        def put(v, x, values):
            for c in range(3):
                fields[v, c, x, own] = values[c]
                ysend_hi[v, c, pl.ds(x - 1, 1)] = values[c][ny - 1 :]
            for slot, c in enumerate((0, 2)):
                ysend_lo[v, slot, pl.ds(x - 1, 1)] = values[c][:1]

        def update_e(v):
            def body(x, carry):
                curls = curl_h(0, x)
                scale = coef[x - 1]
                put(v + 1, x, [fields[v, c, x, own] + scale * curls[c] for c in range(3)])
                return carry

            lax.fori_loop(1, nx + 1, body, 0, unroll=nx)

        def update_adjoint(n, held, v, turn_cos, turn_sin):
            for d in range(dom_len):

                def body(x, total):
                    now = [fields[n, c, x, own] for c in range(3)]
                    drive = envc[0, x - 1] * turn_cos + envc[1, x - 1] * turn_sin
                    driven = [held(c, x) + drive * now[c] for c in range(3)]
                    dot = driven[0] * now[0] + driven[1] * now[1] + driven[2] * now[2]
                    total = total + jnp.where(material[x - 1] == 0, dot, 0.0)
                    curls = curl_h(1, x)
                    scale = coef[x - 1]
                    put(v, x, [driven[c] - scale * curls[c] for c in range(3)])
                    return total

                prods[d] = lax.fori_loop(
                    1 + d * DOMLEN, 1 + (d + 1) * DOMLEN, body, jnp.zeros((ny, nz), jnp.float32), unroll=DOMLEN
                )

        def add_gradient(n):
            norm = 1.0 / math.sqrt(DOMLEN * WBLK * nz)
            sums = jnp.zeros((1, nz), jnp.float32)
            lane_g = lax.broadcasted_iota(jnp.int32, (1, nz), 1)
            for d in range(dom_len):
                for w in range(dom_wid):
                    block = prods[d, pl.ds(w * WBLK, WBLK)]
                    partial = jnp.sum(jnp.sum(block, axis=0, keepdims=True), axis=1, keepdims=True)
                    sums = jnp.where(lane_g == d * dom_wid + w, partial * norm, sums)
            cos_n = jnp.sum(jnp.where(bin_lane == n, cosines, 0.0), axis=1, keepdims=True)
            sin_n = jnp.sum(jnp.where(bin_lane == n, sines, 0.0), axis=1, keepdims=True)
            out_g[pl.ds(0, bins)] = out_g[pl.ds(0, bins)] + cos_n * sums
            out_g[pl.ds(bins, bins)] = out_g[pl.ds(bins, bins)] - sin_n * sums

        def forward(v, carry):
            inner_h(0, v, -COURANT)

            @pl.when(v == 0)
            def _():
                arrive(first_halo())
                pl.when(has_low)(lambda: unpack_h(1))

            arrive(halo(v))
            edge_h(0, v, -COURANT)
            update_e(v)

            @pl.when(v < STEPS - 1)
            def _():
                start(halo(v + 1))

            return carry

        lax.fori_loop(0, STEPS, forward, 0)

        arrive(prefix_copies())
        for c in range(2):
            running = jnp.zeros((ny, nz), jnp.float32)
            for off in range(count - 1, 0, -1):
                running = running + pre[off, c]
            for x in range(nx):
                running = running + signs[x // DOMLEN] * (parity * waves[c][x])
                envc[c, x] = jnp.where(material[x] == 0, running, 0.0)

        update_adjoint(
            STEPS, lambda c, x: fields[VERSIONS, c, x, own], STEPS + 1, math.cos(OMEGA * STEPS), math.sin(OMEGA * STEPS)
        )

        def backward(m, carry):
            v = STEPS + 1 + m
            n = STEPS - 1 - m
            start(halo(v))
            add_gradient(n + 1)
            turn_cos = turn_sin = jnp.float32(0.0)
            for moment in range(1, STEPS):
                turn_cos = jnp.where(n == moment, math.cos(OMEGA * moment), turn_cos)
                turn_sin = jnp.where(n == moment, math.sin(OMEGA * moment), turn_sin)
            inner_h(1, v, COURANT)
            arrive(halo(v))
            edge_h(1, v, COURANT)
            update_adjoint(n, lambda c, x: fields[v, c, x, own], v + 1, turn_cos, turn_sin)
            return carry

        lax.fori_loop(0, STEPS - 1, backward, 0)

        last = VERSIONS - 1
        start(halo(last))
        add_gradient(1)
        for x in range(nx):
            for c in range(3):
                out_e[c, x] = fields[last, c, x + 1, own]
        inner_h(1, last, COURANT)
        arrive(halo(last))
        edge_h(1, last, COURANT)
        for x in range(nx):
            for c in range(3):
                out_h[c, x] = mags[1, c, x + 1, own]

        leave(first_halo())
        leave(prefix_copies())

        def drain(v, carry):
            @pl.when(v != STEPS)
            def _():
                leave(halo(v))

            return carry

        lax.fori_loop(0, VERSIONS, drain, 0)

    f32 = jnp.float32
    vmem = pl.BlockSpec(memory_space=pltpu.VMEM)
    hbm = pl.BlockSpec(memory_space=pl.ANY)
    smem = pl.BlockSpec(memory_space=pltpu.SMEM)
    return pl.pallas_call(
        kernel,
        out_shape=(
            jax.ShapeDtypeStruct((3, nx, ny, nz), f32),
            jax.ShapeDtypeStruct((3, nx, ny, nz), f32),
            jax.ShapeDtypeStruct((2 * bins, nz), f32),
        ),
        in_specs=[hbm, hbm, hbm, hbm, hbm, smem, smem, smem],
        out_specs=(vmem, vmem, vmem),
        scratch_shapes=[
            pltpu.VMEM((VERSIONS + 1, 3, nx + 2, top + 8, nz), f32),
            pltpu.VMEM((2, 3, nx + 1, top, nz), f32),
            pltpu.VMEM((nx, ny, nz), jnp.int32),
            pltpu.VMEM((nx, ny, nz), f32),
            pltpu.VMEM((2, nx, ny, nz), f32),
            pltpu.VMEM((dom_len, ny, nz), f32),
            pltpu.VMEM((count, 2, ny, nz), f32),
            pltpu.VMEM((2, ny, nz), f32),
            pltpu.VMEM((VERSIONS, 3, nx, nz), f32),
            pltpu.VMEM((VERSIONS, 2, nx, nz), f32),
            pltpu.VMEM((VERSIONS, 3, nx, nz), f32),
            pltpu.VMEM((VERSIONS, 2, nx, nz), f32),
            pltpu.VMEM((2, 2, nx, nz), f32),
            pltpu.VMEM((2, 2, nx, nz), f32),
            pltpu.VMEM((nx + 8, nz), f32),
            pltpu.SemaphoreType.DMA((5,)),
            pltpu.SemaphoreType.DMA((VERSIONS, 6)),
            pltpu.SemaphoreType.DMA((VERSIONS, 6)),
            pltpu.SemaphoreType.DMA((3,)),
            pltpu.SemaphoreType.DMA((3,)),
            pltpu.SemaphoreType.DMA((count,)),
            pltpu.SemaphoreType.DMA((count,)),
        ],
        compiler_params=pltpu.CompilerParams(
            collective_id=0, has_side_effects=True, vmem_limit_bytes=48 * 1024 * 1024
        ),
    )


def solution(mesh):
    count, wcount = mesh.shape["len"], mesh.shape["wid"]

    def per_device(ckpt_e, ckpt_h, adj_e, adj_h, material, inv_perm, poling, freqs):
        nx, ny, nz = material.shape
        bins = freqs.shape[0]
        call = make_kernel(count, wcount, nx, ny, nz, bins, inv_perm.shape[0])
        adjoint_e, adjoint_h, grad = call(
            ckpt_e, ckpt_h, adj_e, adj_h, material, inv_perm, poling, freqs
        )
        dom_len, dom_wid = nx // DOMLEN, ny // WBLK
        gradient = grad[:, : dom_len * dom_wid].reshape(2, bins, dom_len, dom_wid)
        return adjoint_e, adjoint_h, gradient

    field = P(None, "len", "wid", None)
    in_specs = (field, field, field, field, P("len", "wid", None), P(), P("len", "wid"), P())
    out_specs = (field, field, P(None, None, "len", "wid"))
    return jax.shard_map(
        per_device, mesh=mesh, in_specs=in_specs, out_specs=out_specs, check_vma=False
    )
```

```python
import math

import jax
import jax.numpy as jnp
from jax import lax
from jax.experimental import pallas as pl
from jax.experimental.pallas import tpu as pltpu
from jax.sharding import PartitionSpec as P

STEPS = 8
DOMLEN = 8
WBLK = 8
COURANT = 0.5
OMEGA = 0.9
MESH = pl.DeviceIdType.MESH
LO = 8
VERSIONS = 2 * STEPS + 1


def zforward(value, lane):
    depth = value.shape[-1]
    return jnp.where(lane < depth - 1, pltpu.roll(value, depth - 1, 1), 0.0)


def zbackward(value, lane):
    return jnp.where(lane > 0, pltpu.roll(value, 1, 1), 0.0)


def make_kernel(count, wcount, nx, ny, nz, bins, nmat):
    top = LO + ny
    dom_len, dom_wid = nx // DOMLEN, ny // WBLK
    span = count * nx

    def kernel(
        ckpt_e, ckpt_h, adj_e, adj_h, cells, inv_perm, poling, freqs,
        out_e, out_h, out_g,
        fields, mags, material, coef, envc, prods, pre, pre_out,
        ysend_hi, ysend_lo, yrecv_lo, yrecv_hi, hsend, hrecv, ypad,
        load_sem, send_sem, recv_sem, hsend_sem, hrecv_sem, psend_sem, precv_sem,
    ):
        me, row = lax.axis_index("len"), lax.axis_index("wid")
        has_prev, has_next = me > 0, me < count - 1
        has_low, has_high = row > 0, row < wcount - 1
        own = pl.ds(LO, ny)

        loads = [
            pltpu.make_async_copy(src, dst, load_sem.at[i])
            for i, (src, dst) in enumerate((
                (ckpt_e, fields.at[0, :, pl.ds(1, nx), own]),
                (ckpt_h, mags.at[0, :, pl.ds(1, nx), own]),
                (adj_h, mags.at[1, :, pl.ds(1, nx), own]),
                (cells, material),
                (adj_e, fields.at[VERSIONS, :, pl.ds(1, nx), own]),
            ))
        ]
        for load in loads:
            load.start()

        for v in range(VERSIONS):
            if v != STEPS:
                fields[v, 0, 0, pl.ds(top, 8)] = jnp.zeros((8, nz), jnp.float32)
                fields[v, 1, nx + 1, pl.ds(0, LO)] = jnp.zeros((LO, nz), jnp.float32)
        pre[...] = jnp.zeros(pre.shape, jnp.float32)
        for h in range(2):
            for c in range(3):
                mags[h, c, 0] = jnp.zeros((top, nz), jnp.float32)
                for x in range(nx):
                    mags[h, c, x + 1, pl.ds(0, LO)] = jnp.zeros((LO, nz), jnp.float32)

        barrier = pltpu.get_barrier_semaphore()

        def greet(there, len_to, wid_to):
            @pl.when(there)
            def _():
                pl.semaphore_signal(
                    barrier, inc=1, device_id={"len": len_to, "wid": wid_to}, device_id_type=MESH
                )

        for off in range(1, count):
            greet(me + off < count, me + off, row)
            greet(me - off >= 0, me - off, row)
        greet(has_low, me, row - 1)
        greet(has_high, me, row + 1)
        greet(has_next & has_low, me + 1, row - 1)
        greet(has_prev & has_high, me - 1, row + 1)

        rows = lax.broadcasted_iota(jnp.int32, (ny, nz), 0)
        signs = []
        for d in range(dom_len):
            sign = jnp.zeros((ny, nz), jnp.float32)
            for w in range(dom_wid):
                value = (2 * poling[d, w] - 1).astype(jnp.float32)
                sign = jnp.where(rows // WBLK == w, value, sign)
            signs.append(sign)
        parity = jnp.float32(1.0)
        if dom_len % 2:
            parity = (1 - 2 * (me % 2)).astype(jnp.float32)
        waves = [
            [f(math.pi * x / DOMLEN) / math.sqrt(span) for x in range(nx)] for f in (math.cos, math.sin)
        ]
        for c in range(2):
            total = jnp.zeros((ny, nz), jnp.float32)
            for d in range(dom_len):
                total = total + signs[d] * sum(waves[c][d * DOMLEN : (d + 1) * DOMLEN])
            pre_out[c] = total * parity

        greeted = (
            (count - 1)
            + has_low.astype(jnp.int32)
            + has_high.astype(jnp.int32)
            + (has_next & has_low).astype(jnp.int32)
            + (has_prev & has_high).astype(jnp.int32)
        )
        pl.semaphore_wait(barrier, greeted)

        def remote(src, dst, send, recv, len_to, wid_to):
            return pltpu.make_async_remote_copy(
                src_ref=src, dst_ref=dst, send_sem=send, recv_sem=recv,
                device_id={"len": len_to, "wid": wid_to}, device_id_type=MESH,
            )

        def halo(v):
            f = fields.at[v]
            pairs = (
                (has_next, has_prev, f.at[:, nx, own], f.at[:, 0, own], me + 1, row),
                (has_prev, has_next, f.at[pl.ds(1, 2), 1, own], f.at[pl.ds(1, 2), nx + 1, own], me - 1, row),
                (has_high, has_low, ysend_hi.at[v], yrecv_lo.at[v], me, row + 1),
                (has_low, has_high, ysend_lo.at[v], yrecv_hi.at[v], me, row - 1),
                (has_next & has_low, has_prev & has_high,
                 f.at[0, nx, pl.ds(LO, 8)], f.at[0, 0, pl.ds(top, 8)], me + 1, row - 1),
                (has_prev & has_high, has_next & has_low,
                 f.at[1, 1, pl.ds(top - 8, 8)], f.at[1, nx + 1, pl.ds(0, LO)], me - 1, row + 1),
            )
            return [
                (sends, gets, remote(src, dst, send_sem.at[v, i], recv_sem.at[v, i], lt, wt))
                for i, (sends, gets, src, dst, lt, wt) in enumerate(pairs)
            ]

        def first_halo():
            pairs = (
                (has_next, has_prev, ckpt_h.at[pl.ds(1, 2), nx - 1], mags.at[0, pl.ds(1, 2), 0, own], me + 1, row),
                (has_next, has_prev, adj_h.at[pl.ds(1, 2), nx - 1], mags.at[1, pl.ds(1, 2), 0, own], me + 1, row),
                (has_high, has_low, hsend, hrecv, me, row + 1),
            )
            return [
                (sends, gets, remote(src, dst, hsend_sem.at[i], hrecv_sem.at[i], lt, wt))
                for i, (sends, gets, src, dst, lt, wt) in enumerate(pairs)
            ]

        def prefix_copies():
            return [
                (me + off < count, me - off >= 0,
                 remote(pre_out, pre.at[off], psend_sem.at[off], precv_sem.at[off], me + off, row))
                for off in range(1, count)
            ]

        def start(copies):
            for sends, _, copy in copies:
                pl.when(sends)(copy.start)

        def len_side(copies):
            return [copies[i] for i in (4, 5, 0, 1)]

        def wid_side(copies):
            return copies[2:4]

        def arrive(copies):
            for _, gets, copy in copies:
                pl.when(gets)(copy.wait_recv)

        def leave(copies):
            for sends, _, copy in copies:
                pl.when(sends)(copy.wait_send)

        for load in loads[:3]:
            load.wait()
        for x in range(nx):
            at, end = pl.ds(x, 1), pl.ds(top - 1, 1)
            for c in range(3):
                ysend_hi[0, c, at] = fields[0, c, x + 1, end]
            for slot, c in enumerate((0, 2)):
                ysend_lo[0, slot, at] = fields[0, c, x + 1, pl.ds(LO, 1)]
                hsend[0, slot, at] = mags[0, c, x + 1, end]
                hsend[1, slot, at] = mags[1, c, x + 1, end]
        start(halo(0))
        start(first_halo())
        start(prefix_copies())

        loads[3].wait()
        loads[4].wait()
        for x in range(nx):
            value = jnp.zeros((ny, nz), jnp.float32)
            for index in range(nmat):
                value = jnp.where(material[x] == index, COURANT * inv_perm[index], value)
            coef[x] = value
        bin_row = lax.broadcasted_iota(jnp.int32, (bins, nz), 0)
        bin_lane = lax.broadcasted_iota(jnp.int32, (bins, nz), 1)
        bin_freq = jnp.zeros((bins, nz), jnp.float32)
        for k in range(bins):
            bin_freq = jnp.where(bin_row == k, freqs[k], bin_freq)
        angles = bin_freq * bin_lane.astype(jnp.float32)
        cosines, sines = jnp.cos(angles), jnp.sin(angles)
        out_g[...] = jnp.zeros(out_g.shape, jnp.float32)

        lane = lax.broadcasted_iota(jnp.int32, (ny, nz), 1)
        lane_x = lax.broadcasted_iota(jnp.int32, (nx, nz), 1)
        above = pl.ds(LO + 1, ny)
        below = pl.ds(LO - 1, ny)

        def curl_e(v, x, ey_x, ez_x):
            ex, ey, ez = (fields[v, c, x, own] for c in range(3))
            ex_y = jnp.where(rows < ny - 1, fields[v, 0, x, above], 0.0)
            ez_y = jnp.where(rows < ny - 1, fields[v, 2, x, above], 0.0)
            return (
                (ez_y - ez) - (zforward(ey, lane) - ey),
                (zforward(ex, lane) - ex) - (ez_x - ez),
                (ey_x - ey) - (ex_y - ex),
            )

        def inner_h(h, v, factor):
            def add(x, curls):
                for c in range(3):
                    mags[h, c, x, own] = mags[h, c, x, own] + factor * curls[c]

            def body(x, carry):
                add(x, curl_e(v, x, fields[v, 1, x + 1, own], fields[v, 2, x + 1, own]))
                return carry

            lax.fori_loop(1, nx, body, 0, unroll=nx - 1)
            zero = jnp.zeros((ny, nz), jnp.float32)
            add(nx, curl_e(v, nx, zero, zero))

        def edge_h(h, v, factor):
            @pl.when(has_next)
            def _():
                mags[h, 1, nx, own] = mags[h, 1, nx, own] - factor * fields[v, 2, nx + 1, own]
                mags[h, 2, nx, own] = mags[h, 2, nx, own] + factor * fields[v, 1, nx + 1, own]

            @pl.when(has_high)
            def _():
                end = pl.ds(top - 1, 1)
                for x in range(nx):
                    at = pl.ds(x, 1)
                    mags[h, 0, x + 1, end] = mags[h, 0, x + 1, end] + factor * yrecv_hi[v, 1, at]
                    mags[h, 2, x + 1, end] = mags[h, 2, x + 1, end] - factor * yrecv_hi[v, 0, at]

            @pl.when(has_prev)
            def _():
                ex, ey, ez = (fields[v, c, 0, own] for c in range(3))
                curl_y = (zforward(ex, lane) - ex) - (fields[v, 2, 1, own] - ez)
                curl_z = (fields[v, 1, 1, own] - ey) - (fields[v, 0, 0, above] - ex)
                mags[h, 1, 0, own] = mags[h, 1, 0, own] + factor * curl_y
                mags[h, 2, 0, own] = mags[h, 2, 0, own] + factor * curl_z

            @pl.when(has_low)
            def _():
                ex, ey, ez = (yrecv_lo[v, c] for c in range(3))
                ypad[pl.ds(0, nx)] = ey
                ypad[pl.ds(nx, 1)] = fields[v, 1, nx + 1, pl.ds(LO - 1, 1)]
                ey_x = ypad[pl.ds(1, nx)]
                curl_x = (ysend_lo[v, 1] - ez) - (zforward(ey, lane_x) - ey)
                curl_z = (ey_x - ey) - (ysend_lo[v, 0] - ex)
                hrecv[h, 0] = hrecv[h, 0] + factor * curl_x
                hrecv[h, 1] = hrecv[h, 1] + factor * curl_z
                unpack_h(h)

        def unpack_h(h):
            for slot, c in enumerate((0, 2)):
                for x in range(nx):
                    mags[h, c, x + 1, pl.ds(LO - 1, 1)] = hrecv[h, slot, pl.ds(x, 1)]

        def curl_h(h, x):
            hx, hy, hz = (mags[h, c, x, own] for c in range(3))
            hx_y, hz_y = mags[h, 0, x, below], mags[h, 2, x, below]
            hy_x, hz_x = mags[h, 1, x - 1, own], mags[h, 2, x - 1, own]
            return (
                (hz - hz_y) - (hy - zbackward(hy, lane)),
                (hx - zbackward(hx, lane)) - (hz - hz_x),
                (hy - hy_x) - (hx - hx_y),
            )

        def put(v, x, values):
            for c in range(3):
                fields[v, c, x, own] = values[c]
                ysend_hi[v, c, pl.ds(x - 1, 1)] = values[c][ny - 1 :]
            for slot, c in enumerate((0, 2)):
                ysend_lo[v, slot, pl.ds(x - 1, 1)] = values[c][:1]

        def update_e(h, source, v, factor, sends):
            def column(x):
                curls = curl_h(h, x)
                scale = coef[x - 1] * factor
                put(v, x, [fields[source, c, x, own] + scale * curls[c] for c in range(3)])

            def body(x, carry):
                column(x)
                return carry

            column(nx)
            column(1)
            sends(len_side)
            lax.fori_loop(2, nx, body, 0, unroll=nx - 2)
            sends(wid_side)

        def inject(n, held, v, turn_cos, turn_sin):
            for d in range(dom_len):

                def body(x, total):
                    now = [fields[n, c, x, own] for c in range(3)]
                    drive = envc[0, x - 1] * turn_cos + envc[1, x - 1] * turn_sin
                    driven = [fields[held, c, x, own] + drive * now[c] for c in range(3)]
                    dot = driven[0] * now[0] + driven[1] * now[1] + driven[2] * now[2]
                    for c in range(3):
                        fields[v, c, x, own] = driven[c]
                    return total + jnp.where(material[x - 1] == 0, dot, 0.0)

                prods[d] = lax.fori_loop(
                    1 + d * DOMLEN, 1 + (d + 1) * DOMLEN, body, jnp.zeros((ny, nz), jnp.float32), unroll=DOMLEN
                )

        def add_gradient(n):
            norm = 1.0 / math.sqrt(DOMLEN * WBLK * nz)
            sums = jnp.zeros((1, nz), jnp.float32)
            lane_g = lax.broadcasted_iota(jnp.int32, (1, nz), 1)
            for d in range(dom_len):
                for w in range(dom_wid):
                    block = prods[d, pl.ds(w * WBLK, WBLK)]
                    partial = jnp.sum(jnp.sum(block, axis=0, keepdims=True), axis=1, keepdims=True)
                    sums = jnp.where(lane_g == d * dom_wid + w, partial * norm, sums)
            cos_n = jnp.sum(jnp.where(bin_lane == n, cosines, 0.0), axis=1, keepdims=True)
            sin_n = jnp.sum(jnp.where(bin_lane == n, sines, 0.0), axis=1, keepdims=True)
            out_g[pl.ds(0, bins)] = out_g[pl.ds(0, bins)] + cos_n * sums
            out_g[pl.ds(bins, bins)] = out_g[pl.ds(bins, bins)] - sin_n * sums

        def envelope():
            for c in range(2):
                running = jnp.zeros((ny, nz), jnp.float32)
                for off in range(count - 1, 0, -1):
                    running = running + pre[off, c]
                for x in range(nx):
                    running = running + signs[x // DOMLEN] * (parity * waves[c][x])
                    envc[c, x] = jnp.where(material[x] == 0, running, 0.0)

        def forward(v, carry):
            @pl.when(v == 2)
            def _():
                arrive(prefix_copies())
                envelope()

            inner_h(0, v, -COURANT)

            @pl.when(v == 0)
            def _():
                arrive(first_halo())
                pl.when(has_low)(lambda: unpack_h(1))

            arrive(halo(v))
            edge_h(0, v, -COURANT)

            def sends(side):
                @pl.when(v < STEPS - 1)
                def _():
                    start(side(halo(v + 1)))

            update_e(0, v, v + 1, 1.0, sends)
            return carry

        lax.fori_loop(0, STEPS, forward, 0)

        inject(STEPS, VERSIONS, STEPS + 1, math.cos(OMEGA * STEPS), math.sin(OMEGA * STEPS))
        update_e(1, STEPS + 1, STEPS + 1, -1.0, lambda side: start(side(halo(STEPS + 1))))

        def backward(m, carry):
            v = STEPS + 1 + m
            n = STEPS - 1 - m
            inner_h(1, v, COURANT)
            add_gradient(n + 1)
            turn_cos = turn_sin = jnp.float32(0.0)
            for moment in range(1, STEPS):
                turn_cos = jnp.where(n == moment, math.cos(OMEGA * moment), turn_cos)
                turn_sin = jnp.where(n == moment, math.sin(OMEGA * moment), turn_sin)
            inject(n, v, v + 1, turn_cos, turn_sin)
            arrive(halo(v))
            edge_h(1, v, COURANT)
            update_e(1, v + 1, v + 1, -1.0, lambda side: start(side(halo(v + 1))))
            return carry

        lax.fori_loop(0, STEPS - 1, backward, 0)

        last = VERSIONS - 1
        add_gradient(1)
        for x in range(nx):
            for c in range(3):
                out_e[c, x] = fields[last, c, x + 1, own]
        inner_h(1, last, COURANT)
        arrive(halo(last))
        edge_h(1, last, COURANT)
        for x in range(nx):
            for c in range(3):
                out_h[c, x] = mags[1, c, x + 1, own]

        leave(first_halo())
        leave(prefix_copies())

        def drain(v, carry):
            @pl.when(v != STEPS)
            def _():
                leave(halo(v))

            return carry

        lax.fori_loop(0, VERSIONS, drain, 0)

    f32 = jnp.float32
    vmem = pl.BlockSpec(memory_space=pltpu.VMEM)
    hbm = pl.BlockSpec(memory_space=pl.ANY)
    smem = pl.BlockSpec(memory_space=pltpu.SMEM)
    return pl.pallas_call(
        kernel,
        out_shape=(
            jax.ShapeDtypeStruct((3, nx, ny, nz), f32),
            jax.ShapeDtypeStruct((3, nx, ny, nz), f32),
            jax.ShapeDtypeStruct((2 * bins, nz), f32),
        ),
        in_specs=[hbm, hbm, hbm, hbm, hbm, smem, smem, smem],
        out_specs=(vmem, vmem, vmem),
        scratch_shapes=[
            pltpu.VMEM((VERSIONS + 1, 3, nx + 2, top + 8, nz), f32),
            pltpu.VMEM((2, 3, nx + 1, top, nz), f32),
            pltpu.VMEM((nx, ny, nz), jnp.int32),
            pltpu.VMEM((nx, ny, nz), f32),
            pltpu.VMEM((2, nx, ny, nz), f32),
            pltpu.VMEM((dom_len, ny, nz), f32),
            pltpu.VMEM((count, 2, ny, nz), f32),
            pltpu.VMEM((2, ny, nz), f32),
            pltpu.VMEM((VERSIONS, 3, nx, nz), f32),
            pltpu.VMEM((VERSIONS, 2, nx, nz), f32),
            pltpu.VMEM((VERSIONS, 3, nx, nz), f32),
            pltpu.VMEM((VERSIONS, 2, nx, nz), f32),
            pltpu.VMEM((2, 2, nx, nz), f32),
            pltpu.VMEM((2, 2, nx, nz), f32),
            pltpu.VMEM((nx + 8, nz), f32),
            pltpu.SemaphoreType.DMA((5,)),
            pltpu.SemaphoreType.DMA((VERSIONS, 6)),
            pltpu.SemaphoreType.DMA((VERSIONS, 6)),
            pltpu.SemaphoreType.DMA((3,)),
            pltpu.SemaphoreType.DMA((3,)),
            pltpu.SemaphoreType.DMA((count,)),
            pltpu.SemaphoreType.DMA((count,)),
        ],
        compiler_params=pltpu.CompilerParams(
            collective_id=0, has_side_effects=True, vmem_limit_bytes=63 * 1024 * 1024
        ),
    )


def solution(mesh):
    count, wcount = mesh.shape["len"], mesh.shape["wid"]

    def per_device(ckpt_e, ckpt_h, adj_e, adj_h, material, inv_perm, poling, freqs):
        nx, ny, nz = material.shape
        bins = freqs.shape[0]
        call = make_kernel(count, wcount, nx, ny, nz, bins, inv_perm.shape[0])
        adjoint_e, adjoint_h, grad = call(
            ckpt_e, ckpt_h, adj_e, adj_h, material, inv_perm, poling, freqs
        )
        dom_len, dom_wid = nx // DOMLEN, ny // WBLK
        gradient = grad[:, : dom_len * dom_wid].reshape(2, bins, dom_len, dom_wid)
        return adjoint_e, adjoint_h, gradient

    field = P(None, "len", "wid", None)
    in_specs = (field, field, field, field, P("len", "wid", None), P(), P("len", "wid"), P())
    out_specs = (field, field, P(None, None, "len", "wid"))
    return jax.shard_map(
        per_device, mesh=mesh, in_specs=in_specs, out_specs=out_specs, check_vma=False
    )
```

```python
import math

import jax
import jax.numpy as jnp
from jax import lax
from jax.experimental import pallas as pl
from jax.experimental.pallas import tpu as pltpu
from jax.sharding import PartitionSpec as P

STEPS = 8
DOMLEN = 8
WBLK = 8
COURANT = 0.5
OMEGA = 0.9
MESH = pl.DeviceIdType.MESH
LO = 8
VERSIONS = 2 * STEPS + 1


def zforward(value, lane):
    depth = value.shape[-1]
    return jnp.where(lane < depth - 1, pltpu.roll(value, depth - 1, 1), 0.0)


def zbackward(value, lane):
    return jnp.where(lane > 0, pltpu.roll(value, 1, 1), 0.0)


def make_kernel(count, wcount, nx, ny, nz, bins, nmat):
    top = LO + ny
    dom_len, dom_wid = nx // DOMLEN, ny // WBLK
    span = count * nx

    def kernel(
        ckpt_e, ckpt_h, adj_e, adj_h, cells, inv_perm, poling, freqs,
        out_e, out_h, out_g,
        fields, mags, material, coef, envc, prods, pre, pre_out,
        ysend_hi, ysend_lo, yrecv_lo, yrecv_hi, hsend, hrecv, ypad, waves_g, coef_rows,
        load_sem, send_sem, recv_sem, hsend_sem, hrecv_sem, psend_sem, precv_sem,
    ):
        me, row = lax.axis_index("len"), lax.axis_index("wid")
        has_prev, has_next = me > 0, me < count - 1
        has_low, has_high = row > 0, row < wcount - 1
        own = pl.ds(LO, ny)

        loads = [
            pltpu.make_async_copy(src, dst, load_sem.at[i])
            for i, (src, dst) in enumerate((
                (ckpt_e, fields.at[0, :, pl.ds(1, nx), own]),
                (ckpt_h, mags.at[0, :, pl.ds(1, nx), own]),
                (adj_h, mags.at[1, :, pl.ds(1, nx), own]),
                (cells, material),
                (adj_e, fields.at[VERSIONS, :, pl.ds(1, nx), own]),
            ))
        ]
        for load in loads:
            load.start()

        for v in range(VERSIONS):
            if v != STEPS:
                fields[v, 0, 0, pl.ds(top, 8)] = jnp.zeros((8, nz), jnp.float32)
                fields[v, 1, nx + 1, pl.ds(0, LO)] = jnp.zeros((LO, nz), jnp.float32)
        pre[...] = jnp.zeros(pre.shape, jnp.float32)
        for h in range(2):
            for c in range(3):
                mags[h, c, 0] = jnp.zeros((top, nz), jnp.float32)
                for x in range(nx):
                    mags[h, c, x + 1, pl.ds(0, LO)] = jnp.zeros((LO, nz), jnp.float32)

        barrier = pltpu.get_barrier_semaphore()

        def greet(there, len_to, wid_to):
            @pl.when(there)
            def _():
                pl.semaphore_signal(
                    barrier, inc=1, device_id={"len": len_to, "wid": wid_to}, device_id_type=MESH
                )

        for off in range(1, count):
            greet(me + off < count, me + off, row)
            greet(me - off >= 0, me - off, row)
        greet(has_low, me, row - 1)
        greet(has_high, me, row + 1)
        greet(has_next & has_low, me + 1, row - 1)
        greet(has_prev & has_high, me - 1, row + 1)

        rows = lax.broadcasted_iota(jnp.int32, (ny, nz), 0)
        signs = []
        for d in range(dom_len):
            sign = jnp.zeros((ny, nz), jnp.float32)
            for w in range(dom_wid):
                value = (2 * poling[d, w] - 1).astype(jnp.float32)
                sign = jnp.where(rows // WBLK == w, value, sign)
            signs.append(sign)
        parity = jnp.float32(1.0)
        if dom_len % 2:
            parity = (1 - 2 * (me % 2)).astype(jnp.float32)
        waves = [
            [f(math.pi * x / DOMLEN) / math.sqrt(span) for x in range(nx)] for f in (math.cos, math.sin)
        ]
        for c in range(2):
            total = jnp.zeros((ny, nz), jnp.float32)
            for d in range(dom_len):
                total = total + signs[d] * sum(waves[c][d * DOMLEN : (d + 1) * DOMLEN])
            pre_out[c] = total * parity

        greeted = (
            (count - 1)
            + has_low.astype(jnp.int32)
            + has_high.astype(jnp.int32)
            + (has_next & has_low).astype(jnp.int32)
            + (has_prev & has_high).astype(jnp.int32)
        )
        pl.semaphore_wait(barrier, greeted)

        def remote(src, dst, send, recv, len_to, wid_to):
            return pltpu.make_async_remote_copy(
                src_ref=src, dst_ref=dst, send_sem=send, recv_sem=recv,
                device_id={"len": len_to, "wid": wid_to}, device_id_type=MESH,
            )

        def halo(v):
            f = fields.at[v]
            pairs = (
                (has_next, has_prev, f.at[:, nx, own], f.at[:, 0, own], me + 1, row),
                (has_prev, has_next, f.at[pl.ds(1, 2), 1, own], f.at[pl.ds(1, 2), nx + 1, own], me - 1, row),
                (has_high, has_low, ysend_hi.at[v], yrecv_lo.at[v], me, row + 1),
                (has_low, has_high, ysend_lo.at[v], yrecv_hi.at[v], me, row - 1),
                (has_next & has_low, has_prev & has_high,
                 f.at[0, nx, pl.ds(LO, 8)], f.at[0, 0, pl.ds(top, 8)], me + 1, row - 1),
                (has_prev & has_high, has_next & has_low,
                 f.at[1, 1, pl.ds(top - 8, 8)], f.at[1, nx + 1, pl.ds(0, LO)], me - 1, row + 1),
            )
            return [
                (sends, gets, remote(src, dst, send_sem.at[v, i], recv_sem.at[v, i], lt, wt))
                for i, (sends, gets, src, dst, lt, wt) in enumerate(pairs)
            ]

        def first_halo():
            pairs = (
                (has_next, has_prev, ckpt_h.at[pl.ds(1, 2), nx - 1], mags.at[0, pl.ds(1, 2), 0, own], me + 1, row),
                (has_next, has_prev, adj_h.at[pl.ds(1, 2), nx - 1], mags.at[1, pl.ds(1, 2), 0, own], me + 1, row),
                (has_high, has_low, hsend, hrecv, me, row + 1),
            )
            return [
                (sends, gets, remote(src, dst, hsend_sem.at[i], hrecv_sem.at[i], lt, wt))
                for i, (sends, gets, src, dst, lt, wt) in enumerate(pairs)
            ]

        def prefix_copies():
            return [
                (me + off < count, me - off >= 0,
                 remote(pre_out, pre.at[off], psend_sem.at[off], precv_sem.at[off], me + off, row))
                for off in range(1, count)
            ]

        def start(copies):
            for sends, _, copy in copies:
                pl.when(sends)(copy.start)

        def arrive(copies):
            for _, gets, copy in copies:
                pl.when(gets)(copy.wait_recv)

        def leave(copies):
            for sends, _, copy in copies:
                pl.when(sends)(copy.wait_send)

        for load in loads[:3]:
            load.wait()
        for x in range(nx):
            at, end = pl.ds(x, 1), pl.ds(top - 1, 1)
            for c in range(3):
                ysend_hi[0, c, at] = fields[0, c, x + 1, end]
            for slot, c in enumerate((0, 2)):
                ysend_lo[0, slot, at] = fields[0, c, x + 1, pl.ds(LO, 1)]
                hsend[0, slot, at] = mags[0, c, x + 1, end]
                hsend[1, slot, at] = mags[1, c, x + 1, end]
        start(halo(0))
        start(first_halo())
        start(prefix_copies())

        loads[3].wait()
        loads[4].wait()
        for x in range(nx):
            value = jnp.zeros((ny, nz), jnp.float32)
            for index in range(nmat):
                value = jnp.where(material[x] == index, COURANT * inv_perm[index], value)
            coef[x] = value
            coef_rows[0, pl.ds(x, 1)] = value[:1]
            coef_rows[1, pl.ds(x, 1)] = value[ny - 1 :]
        bin_row = lax.broadcasted_iota(jnp.int32, (STEPS, nz), 0)
        bin_lane = lax.broadcasted_iota(jnp.int32, (STEPS, nz), 1)
        bin_freq = jnp.zeros((STEPS, nz), jnp.float32)
        for k in range(bins):
            bin_freq = jnp.where(bin_lane == k, freqs[k], bin_freq)
        angles = bin_freq * (bin_row + 1).astype(jnp.float32)
        waves_g[0], waves_g[1] = jnp.cos(angles), -jnp.sin(angles)
        out_g[...] = jnp.zeros(out_g.shape, jnp.float32)

        lane = lax.broadcasted_iota(jnp.int32, (ny, nz), 1)
        lane_x = lax.broadcasted_iota(jnp.int32, (nx, nz), 1)
        rows_x = lax.broadcasted_iota(jnp.int32, (nx, nz), 0)
        above = pl.ds(LO + 1, ny)
        below = pl.ds(LO - 1, ny)

        def curl_e(v, x, ey_x, ez_x):
            ex, ey, ez = (fields[v, c, x, own] for c in range(3))
            ex_y = jnp.where(rows < ny - 1, fields[v, 0, x, above], 0.0)
            ez_y = jnp.where(rows < ny - 1, fields[v, 2, x, above], 0.0)
            return (
                (ez_y - ez) - (zforward(ey, lane) - ey),
                (zforward(ex, lane) - ex) - (ez_x - ez),
                (ey_x - ey) - (ex_y - ex),
            )

        def inner_h(h, v, factor):
            def add(x, curls):
                for c in range(3):
                    mags[h, c, x, own] = mags[h, c, x, own] + factor * curls[c]

            def body(x, carry):
                add(x, curl_e(v, x, fields[v, 1, x + 1, own], fields[v, 2, x + 1, own]))
                return carry

            lax.fori_loop(1, nx, body, 0, unroll=nx - 1)
            zero = jnp.zeros((ny, nz), jnp.float32)
            add(nx, curl_e(v, nx, zero, zero))

        def edge_h(h, v, factor):
            @pl.when(has_next)
            def _():
                mags[h, 1, nx, own] = mags[h, 1, nx, own] - factor * fields[v, 2, nx + 1, own]
                mags[h, 2, nx, own] = mags[h, 2, nx, own] + factor * fields[v, 1, nx + 1, own]

            @pl.when(has_high)
            def _():
                end = pl.ds(top - 1, 1)
                for x in range(nx):
                    at = pl.ds(x, 1)
                    mags[h, 0, x + 1, end] = mags[h, 0, x + 1, end] + factor * yrecv_hi[v, 1, at]
                    mags[h, 2, x + 1, end] = mags[h, 2, x + 1, end] - factor * yrecv_hi[v, 0, at]

            @pl.when(has_prev)
            def _():
                ex, ey, ez = (fields[v, c, 0, own] for c in range(3))
                curl_y = (zforward(ex, lane) - ex) - (fields[v, 2, 1, own] - ez)
                curl_z = (fields[v, 1, 1, own] - ey) - (fields[v, 0, 0, above] - ex)
                mags[h, 1, 0, own] = mags[h, 1, 0, own] + factor * curl_y
                mags[h, 2, 0, own] = mags[h, 2, 0, own] + factor * curl_z

            @pl.when(has_low)
            def _():
                ex, ey, ez = (yrecv_lo[v, c] for c in range(3))
                ypad[pl.ds(0, nx)] = ey
                ypad[pl.ds(nx, 1)] = fields[v, 1, nx + 1, pl.ds(LO - 1, 1)]
                ey_x = ypad[pl.ds(1, nx)]
                curl_x = (ysend_lo[v, 1] - ez) - (zforward(ey, lane_x) - ey)
                curl_z = (ey_x - ey) - (ysend_lo[v, 0] - ex)
                hrecv[h, 0] = hrecv[h, 0] + factor * curl_x
                hrecv[h, 1] = hrecv[h, 1] + factor * curl_z
                unpack_h(h)

        def unpack_h(h):
            for slot, c in enumerate((0, 2)):
                for x in range(nx):
                    mags[h, c, x + 1, pl.ds(LO - 1, 1)] = hrecv[h, slot, pl.ds(x, 1)]

        def curl_h(h, x):
            hx, hy, hz = (mags[h, c, x, own] for c in range(3))
            hx_y, hz_y = mags[h, 0, x, below], mags[h, 2, x, below]
            hy_x, hz_x = mags[h, 1, x - 1, own], mags[h, 2, x - 1, own]
            return (
                (hz - hz_y) - (hy - zbackward(hy, lane)),
                (hx - zbackward(hx, lane)) - (hz - hz_x),
                (hy - hy_x) - (hx - hx_y),
            )

        def put(v, x, values):
            for c in range(3):
                fields[v, c, x, own] = values[c]
                ysend_hi[v, c, pl.ds(x - 1, 1)] = values[c][ny - 1 :]
            for slot, c in enumerate((0, 2)):
                ysend_lo[v, slot, pl.ds(x - 1, 1)] = values[c][:1]

        def update_e(h, source, v, factor):
            def body(x, carry):
                curls = curl_h(h, x)
                scale = coef[x - 1] * factor
                put(v, x, [fields[source, c, x, own] + scale * curls[c] for c in range(3)])
                return carry

            lax.fori_loop(1, nx + 1, body, 0, unroll=nx)

        def edge_e(h, v, factor, new, factor_e):
            @pl.when(has_next)
            def _():
                dy, dz = -factor * fields[v, 2, nx + 1, own], factor * fields[v, 1, nx + 1, own]
                mags[h, 1, nx, own] = mags[h, 1, nx, own] + dy
                mags[h, 2, nx, own] = mags[h, 2, nx, own] + dz
                dz_y = jnp.where(rows > 0, pltpu.roll(dz, 1, 0), 0.0)
                scale = coef[nx - 1] * factor_e
                curls = ((dz - dz_y) - (dy - zbackward(dy, lane)), -dz, dy)
                for c in range(3):
                    fields[new, c, nx, own] = fields[new, c, nx, own] + scale * curls[c]

            @pl.when(has_prev)
            def _():
                ex, ey, ez = (fields[v, c, 0, own] for c in range(3))
                dy = factor * ((zforward(ex, lane) - ex) - (fields[v, 2, 1, own] - ez))
                dz = factor * ((fields[v, 1, 1, own] - ey) - (fields[v, 0, 0, above] - ex))
                mags[h, 1, 0, own] = mags[h, 1, 0, own] + dy
                mags[h, 2, 0, own] = mags[h, 2, 0, own] + dz
                scale = coef[0] * factor_e
                fields[new, 1, 1, own] = fields[new, 1, 1, own] + scale * dz
                fields[new, 2, 1, own] = fields[new, 2, 1, own] - scale * dy

            end, begin = pl.ds(top - 1, 1), pl.ds(LO, 1)
            for x in (0, nx - 1):
                for c in range(3):
                    ysend_hi[new, c, pl.ds(x, 1)] = fields[new, c, x + 1, end]
                for slot, c in enumerate((0, 2)):
                    ysend_lo[new, slot, pl.ds(x, 1)] = fields[new, c, x + 1, begin]

            @pl.when(has_high)
            def _():
                dx, dz = factor * yrecv_hi[v, 1], -factor * yrecv_hi[v, 0]
                dz_x = jnp.where(rows_x > 0, pltpu.roll(dz, 1, 0), 0.0)
                scale = coef_rows[1] * factor_e
                curls = (dz, (dx - zbackward(dx, lane_x)) - (dz - dz_x), -dx)
                for c in range(3):
                    ysend_hi[new, c] = ysend_hi[new, c] + scale * curls[c]
                for c in range(3):
                    for x in range(nx):
                        fields[new, c, x + 1, end] = ysend_hi[new, c, pl.ds(x, 1)]

            @pl.when(has_low)
            def _():
                ex, ey, ez = (yrecv_lo[v, c] for c in range(3))
                ypad[pl.ds(0, nx)] = ey
                ypad[pl.ds(nx, 1)] = fields[v, 1, nx + 1, pl.ds(LO - 1, 1)]
                ey_x = ypad[pl.ds(1, nx)]
                dx = factor * ((ysend_lo[v, 1] - ez) - (zforward(ey, lane_x) - ey))
                dz = factor * ((ey_x - ey) - (ysend_lo[v, 0] - ex))
                hrecv[h, 0] = hrecv[h, 0] + dx
                hrecv[h, 1] = hrecv[h, 1] + dz
                scale = coef_rows[0] * factor_e
                ysend_lo[new, 0] = ysend_lo[new, 0] - scale * dz
                ysend_lo[new, 1] = ysend_lo[new, 1] + scale * dx
                for slot, c in enumerate((0, 2)):
                    for x in range(nx):
                        fields[new, c, x + 1, begin] = ysend_lo[new, slot, pl.ds(x, 1)]

        def edge_rows(h, v, factor):
            @pl.when(has_high)
            def _():
                end = pl.ds(top - 1, 1)
                for x in range(nx):
                    at = pl.ds(x, 1)
                    mags[h, 0, x + 1, end] = mags[h, 0, x + 1, end] + factor * yrecv_hi[v, 1, at]
                    mags[h, 2, x + 1, end] = mags[h, 2, x + 1, end] - factor * yrecv_hi[v, 0, at]

            pl.when(has_low)(lambda: unpack_h(h))

        def inject(n, held, v, turn_cos, turn_sin):
            for d in range(dom_len):

                def body(x, total):
                    now = [fields[n, c, x, own] for c in range(3)]
                    drive = envc[0, x - 1] * turn_cos + envc[1, x - 1] * turn_sin
                    driven = [fields[held, c, x, own] + drive * now[c] for c in range(3)]
                    dot = driven[0] * now[0] + driven[1] * now[1] + driven[2] * now[2]
                    for c in range(3):
                        fields[v, c, x, own] = driven[c]
                    return total + jnp.where(material[x - 1] == 0, dot, 0.0)

                prods[d] = lax.fori_loop(
                    1 + d * DOMLEN, 1 + (d + 1) * DOMLEN, body, jnp.zeros((ny, nz), jnp.float32), unroll=DOMLEN
                )

        def add_gradient(n):
            norm = 1.0 / math.sqrt(DOMLEN * WBLK * nz)
            at = pl.ds(n - 1, 1)
            for d in range(dom_len):
                for w in range(dom_wid):
                    block = prods[d, pl.ds(w * WBLK, WBLK)]
                    partial = jnp.sum(jnp.sum(block, axis=0, keepdims=True), axis=1, keepdims=True) * norm
                    for c in range(2):
                        term = (waves_g[c, at] * partial)[:, :bins]
                        out_g[c, d, pl.ds(w, 1)] = out_g[c, d, pl.ds(w, 1)] + term

        def envelope():
            for c in range(2):
                running = jnp.zeros((ny, nz), jnp.float32)
                for off in range(count - 1, 0, -1):
                    running = running + pre[off, c]
                for x in range(nx):
                    running = running + signs[x // DOMLEN] * (parity * waves[c][x])
                    envc[c, x] = jnp.where(material[x] == 0, running, 0.0)

        def forward(v, carry):
            @pl.when(v == 2)
            def _():
                arrive(prefix_copies())
                envelope()

            inner_h(0, v, -COURANT)

            @pl.when(v == 0)
            def _():
                arrive(first_halo())

                @pl.when(has_low)
                def _():
                    unpack_h(0)
                    unpack_h(1)

            update_e(0, v, v + 1, 1.0)
            arrive(halo(v))
            edge_e(0, v, -COURANT, v + 1, 1.0)

            @pl.when(v < STEPS - 1)
            def _():
                start(halo(v + 1))

            edge_rows(0, v, -COURANT)
            return carry

        lax.fori_loop(0, STEPS, forward, 0)

        inject(STEPS, VERSIONS, STEPS + 1, math.cos(OMEGA * STEPS), math.sin(OMEGA * STEPS))
        update_e(1, STEPS + 1, STEPS + 1, -1.0)
        start(halo(STEPS + 1))

        def backward(m, carry):
            v = STEPS + 1 + m
            n = STEPS - 1 - m
            inner_h(1, v, COURANT)
            add_gradient(n + 1)
            turn_cos = turn_sin = jnp.float32(0.0)
            for moment in range(1, STEPS):
                turn_cos = jnp.where(n == moment, math.cos(OMEGA * moment), turn_cos)
                turn_sin = jnp.where(n == moment, math.sin(OMEGA * moment), turn_sin)
            inject(n, v, v + 1, turn_cos, turn_sin)
            update_e(1, v + 1, v + 1, -1.0)
            arrive(halo(v))
            edge_e(1, v, COURANT, v + 1, -1.0)
            start(halo(v + 1))
            edge_rows(1, v, COURANT)
            return carry

        lax.fori_loop(0, STEPS - 1, backward, 0)

        last = VERSIONS - 1
        add_gradient(1)
        for x in range(nx):
            for c in range(3):
                out_e[c, x] = fields[last, c, x + 1, own]
        inner_h(1, last, COURANT)
        arrive(halo(last))
        edge_h(1, last, COURANT)
        for x in range(nx):
            for c in range(3):
                out_h[c, x] = mags[1, c, x + 1, own]

        leave(first_halo())
        leave(prefix_copies())

        def drain(v, carry):
            @pl.when(v != STEPS)
            def _():
                leave(halo(v))

            return carry

        lax.fori_loop(0, VERSIONS, drain, 0)

    f32 = jnp.float32
    vmem = pl.BlockSpec(memory_space=pltpu.VMEM)
    hbm = pl.BlockSpec(memory_space=pl.ANY)
    smem = pl.BlockSpec(memory_space=pltpu.SMEM)
    return pl.pallas_call(
        kernel,
        out_shape=(
            jax.ShapeDtypeStruct((3, nx, ny, nz), f32),
            jax.ShapeDtypeStruct((3, nx, ny, nz), f32),
            jax.ShapeDtypeStruct((2, dom_len, dom_wid, bins), f32),
        ),
        in_specs=[hbm, hbm, hbm, hbm, hbm, smem, smem, smem],
        out_specs=(vmem, vmem, vmem),
        scratch_shapes=[
            pltpu.VMEM((VERSIONS + 1, 3, nx + 2, top + 8, nz), f32),
            pltpu.VMEM((2, 3, nx + 1, top, nz), f32),
            pltpu.VMEM((nx, ny, nz), jnp.int32),
            pltpu.VMEM((nx, ny, nz), f32),
            pltpu.VMEM((2, nx, ny, nz), f32),
            pltpu.VMEM((dom_len, ny, nz), f32),
            pltpu.VMEM((count, 2, ny, nz), f32),
            pltpu.VMEM((2, ny, nz), f32),
            pltpu.VMEM((VERSIONS, 3, nx, nz), f32),
            pltpu.VMEM((VERSIONS, 2, nx, nz), f32),
            pltpu.VMEM((VERSIONS, 3, nx, nz), f32),
            pltpu.VMEM((VERSIONS, 2, nx, nz), f32),
            pltpu.VMEM((2, 2, nx, nz), f32),
            pltpu.VMEM((2, 2, nx, nz), f32),
            pltpu.VMEM((nx + 8, nz), f32),
            pltpu.VMEM((2, STEPS, nz), f32),
            pltpu.VMEM((2, nx, nz), f32),
            pltpu.SemaphoreType.DMA((5,)),
            pltpu.SemaphoreType.DMA((VERSIONS, 6)),
            pltpu.SemaphoreType.DMA((VERSIONS, 6)),
            pltpu.SemaphoreType.DMA((3,)),
            pltpu.SemaphoreType.DMA((3,)),
            pltpu.SemaphoreType.DMA((count,)),
            pltpu.SemaphoreType.DMA((count,)),
        ],
        compiler_params=pltpu.CompilerParams(
            collective_id=0, has_side_effects=True, vmem_limit_bytes=63 * 1024 * 1024
        ),
    )


def solution(mesh):
    count, wcount = mesh.shape["len"], mesh.shape["wid"]

    def per_device(ckpt_e, ckpt_h, adj_e, adj_h, material, inv_perm, poling, freqs):
        nx, ny, nz = material.shape
        bins = freqs.shape[0]
        call = make_kernel(count, wcount, nx, ny, nz, bins, inv_perm.shape[0])
        adjoint_e, adjoint_h, grad = call(
            ckpt_e, ckpt_h, adj_e, adj_h, material, inv_perm, poling, freqs
        )
        gradient = jnp.transpose(grad, (0, 3, 1, 2))
        return adjoint_e, adjoint_h, gradient

    field = P(None, "len", "wid", None)
    in_specs = (field, field, field, field, P("len", "wid", None), P(), P("len", "wid"), P())
    out_specs = (field, field, P(None, None, "len", "wid"))
    return jax.shard_map(
        per_device, mesh=mesh, in_specs=in_specs, out_specs=out_specs, check_vma=False
    )
```

```python
import math

import jax
import jax.numpy as jnp
from jax import lax
from jax.experimental import pallas as pl
from jax.experimental.pallas import tpu as pltpu
from jax.sharding import PartitionSpec as P

STEPS = 8
DOMLEN = 8
WBLK = 8
COURANT = 0.5
OMEGA = 0.9
MESH = pl.DeviceIdType.MESH
LO = 8
VERSIONS = 2 * STEPS + 1


def zforward(value, lane):
    depth = value.shape[-1]
    return jnp.where(lane < depth - 1, pltpu.roll(value, depth - 1, 1), 0.0)


def zbackward(value, lane):
    return jnp.where(lane > 0, pltpu.roll(value, 1, 1), 0.0)


def make_kernel(count, wcount, nx, ny, nz, bins, nmat):
    top = LO + ny
    dom_len, dom_wid = nx // DOMLEN, ny // WBLK
    span = count * nx

    def kernel(
        ckpt_e, ckpt_h, adj_e, adj_h, cells, inv_perm, poling, freqs,
        out_e, out_h, out_g,
        fields, mags, material, coef, envc, prods, pre, pre_out,
        ysend_hi, ysend_lo, yrecv_lo, yrecv_hi, hsend, hrecv, ypad, waves_g,
        load_sem, send_sem, recv_sem, hsend_sem, hrecv_sem, psend_sem, precv_sem,
    ):
        me, row = lax.axis_index("len"), lax.axis_index("wid")
        has_prev, has_next = me > 0, me < count - 1
        has_low, has_high = row > 0, row < wcount - 1
        own = pl.ds(LO, ny)

        loads = [
            pltpu.make_async_copy(src, dst, load_sem.at[i])
            for i, (src, dst) in enumerate((
                (ckpt_e, fields.at[0, :, pl.ds(1, nx), own]),
                (ckpt_h, mags.at[0, :, pl.ds(1, nx), own]),
                (adj_h, mags.at[1, :, pl.ds(1, nx), own]),
                (cells, material),
                (adj_e, fields.at[VERSIONS, :, pl.ds(1, nx), own]),
            ))
        ]
        for load in loads:
            load.start()

        for v in range(VERSIONS):
            if v != STEPS:
                fields[v, 0, 0, pl.ds(top, 8)] = jnp.zeros((8, nz), jnp.float32)
                fields[v, 1, nx + 1, pl.ds(0, LO)] = jnp.zeros((LO, nz), jnp.float32)
        pre[...] = jnp.zeros(pre.shape, jnp.float32)
        for h in range(2):
            for c in range(3):
                mags[h, c, 0] = jnp.zeros((top, nz), jnp.float32)
                for x in range(nx):
                    mags[h, c, x + 1, pl.ds(0, LO)] = jnp.zeros((LO, nz), jnp.float32)

        barrier = pltpu.get_barrier_semaphore()

        def greet(there, len_to, wid_to):
            @pl.when(there)
            def _():
                pl.semaphore_signal(
                    barrier, inc=1, device_id={"len": len_to, "wid": wid_to}, device_id_type=MESH
                )

        for off in range(1, count):
            greet(me + off < count, me + off, row)
            greet(me - off >= 0, me - off, row)
        greet(has_low, me, row - 1)
        greet(has_high, me, row + 1)
        greet(has_next & has_low, me + 1, row - 1)
        greet(has_prev & has_high, me - 1, row + 1)

        rows = lax.broadcasted_iota(jnp.int32, (ny, nz), 0)
        signs = []
        for d in range(dom_len):
            sign = jnp.zeros((ny, nz), jnp.float32)
            for w in range(dom_wid):
                value = (2 * poling[d, w] - 1).astype(jnp.float32)
                sign = jnp.where(rows // WBLK == w, value, sign)
            signs.append(sign)
        parity = jnp.float32(1.0)
        if dom_len % 2:
            parity = (1 - 2 * (me % 2)).astype(jnp.float32)
        waves = [
            [f(math.pi * x / DOMLEN) / math.sqrt(span) for x in range(nx)] for f in (math.cos, math.sin)
        ]
        for c in range(2):
            total = jnp.zeros((ny, nz), jnp.float32)
            for d in range(dom_len):
                total = total + signs[d] * sum(waves[c][d * DOMLEN : (d + 1) * DOMLEN])
            pre_out[c] = total * parity

        greeted = (
            (count - 1)
            + has_low.astype(jnp.int32)
            + has_high.astype(jnp.int32)
            + (has_next & has_low).astype(jnp.int32)
            + (has_prev & has_high).astype(jnp.int32)
        )
        pl.semaphore_wait(barrier, greeted)

        def remote(src, dst, send, recv, len_to, wid_to):
            return pltpu.make_async_remote_copy(
                src_ref=src, dst_ref=dst, send_sem=send, recv_sem=recv,
                device_id={"len": len_to, "wid": wid_to}, device_id_type=MESH,
            )

        def halo(v):
            f = fields.at[v]
            pairs = (
                (has_next, has_prev, f.at[:, nx, own], f.at[:, 0, own], me + 1, row),
                (has_prev, has_next, f.at[pl.ds(1, 2), 1, own], f.at[pl.ds(1, 2), nx + 1, own], me - 1, row),
                (has_high, has_low, ysend_hi.at[v], yrecv_lo.at[v], me, row + 1),
                (has_low, has_high, ysend_lo.at[v], yrecv_hi.at[v], me, row - 1),
                (has_next & has_low, has_prev & has_high,
                 f.at[0, nx, pl.ds(LO, 8)], f.at[0, 0, pl.ds(top, 8)], me + 1, row - 1),
                (has_prev & has_high, has_next & has_low,
                 f.at[1, 1, pl.ds(top - 8, 8)], f.at[1, nx + 1, pl.ds(0, LO)], me - 1, row + 1),
            )
            return [
                (sends, gets, remote(src, dst, send_sem.at[v, i], recv_sem.at[v, i], lt, wt))
                for i, (sends, gets, src, dst, lt, wt) in enumerate(pairs)
            ]

        def first_halo():
            pairs = (
                (has_next, has_prev, ckpt_h.at[pl.ds(1, 2), nx - 1], mags.at[0, pl.ds(1, 2), 0, own], me + 1, row),
                (has_next, has_prev, adj_h.at[pl.ds(1, 2), nx - 1], mags.at[1, pl.ds(1, 2), 0, own], me + 1, row),
                (has_high, has_low, hsend, hrecv, me, row + 1),
            )
            return [
                (sends, gets, remote(src, dst, hsend_sem.at[i], hrecv_sem.at[i], lt, wt))
                for i, (sends, gets, src, dst, lt, wt) in enumerate(pairs)
            ]

        def prefix_copies():
            return [
                (me + off < count, me - off >= 0,
                 remote(pre_out, pre.at[off], psend_sem.at[off], precv_sem.at[off], me + off, row))
                for off in range(1, count)
            ]

        def start(copies):
            for sends, _, copy in copies:
                pl.when(sends)(copy.start)

        def len_side(copies):
            return [copies[i] for i in (4, 5, 0, 1)]

        def wid_side(copies):
            return copies[2:4]

        def arrive(copies):
            for _, gets, copy in copies:
                pl.when(gets)(copy.wait_recv)

        def leave(copies):
            for sends, _, copy in copies:
                pl.when(sends)(copy.wait_send)

        for load in loads[:3]:
            load.wait()
        for x in range(nx):
            at, end = pl.ds(x, 1), pl.ds(top - 1, 1)
            for c in range(3):
                ysend_hi[0, c, at] = fields[0, c, x + 1, end]
            for slot, c in enumerate((0, 2)):
                ysend_lo[0, slot, at] = fields[0, c, x + 1, pl.ds(LO, 1)]
                hsend[0, slot, at] = mags[0, c, x + 1, end]
                hsend[1, slot, at] = mags[1, c, x + 1, end]
        start(halo(0))
        start(first_halo())
        start(prefix_copies())

        loads[3].wait()
        loads[4].wait()
        for x in range(nx):
            value = jnp.zeros((ny, nz), jnp.float32)
            for index in range(nmat):
                value = jnp.where(material[x] == index, COURANT * inv_perm[index], value)
            coef[x] = value
        bin_row = lax.broadcasted_iota(jnp.int32, (STEPS, nz), 0)
        bin_lane = lax.broadcasted_iota(jnp.int32, (STEPS, nz), 1)
        bin_freq = jnp.zeros((STEPS, nz), jnp.float32)
        for k in range(bins):
            bin_freq = jnp.where(bin_lane == k, freqs[k], bin_freq)
        angles = bin_freq * (bin_row + 1).astype(jnp.float32)
        waves_g[0], waves_g[1] = jnp.cos(angles), -jnp.sin(angles)
        out_g[...] = jnp.zeros(out_g.shape, jnp.float32)

        lane = lax.broadcasted_iota(jnp.int32, (ny, nz), 1)
        lane_x = lax.broadcasted_iota(jnp.int32, (nx, nz), 1)
        above = pl.ds(LO + 1, ny)
        below = pl.ds(LO - 1, ny)

        def curl_e(v, x, ey_x, ez_x):
            ex, ey, ez = (fields[v, c, x, own] for c in range(3))
            ex_y = jnp.where(rows < ny - 1, fields[v, 0, x, above], 0.0)
            ez_y = jnp.where(rows < ny - 1, fields[v, 2, x, above], 0.0)
            return (
                (ez_y - ez) - (zforward(ey, lane) - ey),
                (zforward(ex, lane) - ex) - (ez_x - ez),
                (ey_x - ey) - (ex_y - ex),
            )

        def inner_h(h, v, factor):
            def add(x, curls):
                for c in range(3):
                    mags[h, c, x, own] = mags[h, c, x, own] + factor * curls[c]

            def body(x, carry):
                add(x, curl_e(v, x, fields[v, 1, x + 1, own], fields[v, 2, x + 1, own]))
                return carry

            lax.fori_loop(1, nx, body, 0, unroll=nx - 1)
            zero = jnp.zeros((ny, nz), jnp.float32)
            add(nx, curl_e(v, nx, zero, zero))

        def edge_h(h, v, factor):
            @pl.when(has_next)
            def _():
                mags[h, 1, nx, own] = mags[h, 1, nx, own] - factor * fields[v, 2, nx + 1, own]
                mags[h, 2, nx, own] = mags[h, 2, nx, own] + factor * fields[v, 1, nx + 1, own]

            @pl.when(has_high)
            def _():
                end = pl.ds(top - 1, 1)
                for x in range(nx):
                    at = pl.ds(x, 1)
                    mags[h, 0, x + 1, end] = mags[h, 0, x + 1, end] + factor * yrecv_hi[v, 1, at]
                    mags[h, 2, x + 1, end] = mags[h, 2, x + 1, end] - factor * yrecv_hi[v, 0, at]

            @pl.when(has_prev)
            def _():
                ex, ey, ez = (fields[v, c, 0, own] for c in range(3))
                curl_y = (zforward(ex, lane) - ex) - (fields[v, 2, 1, own] - ez)
                curl_z = (fields[v, 1, 1, own] - ey) - (fields[v, 0, 0, above] - ex)
                mags[h, 1, 0, own] = mags[h, 1, 0, own] + factor * curl_y
                mags[h, 2, 0, own] = mags[h, 2, 0, own] + factor * curl_z

            @pl.when(has_low)
            def _():
                ex, ey, ez = (yrecv_lo[v, c] for c in range(3))
                ypad[pl.ds(0, nx)] = ey
                ypad[pl.ds(nx, 1)] = fields[v, 1, nx + 1, pl.ds(LO - 1, 1)]
                ey_x = ypad[pl.ds(1, nx)]
                curl_x = (ysend_lo[v, 1] - ez) - (zforward(ey, lane_x) - ey)
                curl_z = (ey_x - ey) - (ysend_lo[v, 0] - ex)
                hrecv[h, 0] = hrecv[h, 0] + factor * curl_x
                hrecv[h, 1] = hrecv[h, 1] + factor * curl_z
                unpack_h(h)

        def unpack_h(h):
            for slot, c in enumerate((0, 2)):
                for x in range(nx):
                    mags[h, c, x + 1, pl.ds(LO - 1, 1)] = hrecv[h, slot, pl.ds(x, 1)]

        def curl_h(h, x):
            hx, hy, hz = (mags[h, c, x, own] for c in range(3))
            hx_y, hz_y = mags[h, 0, x, below], mags[h, 2, x, below]
            hy_x, hz_x = mags[h, 1, x - 1, own], mags[h, 2, x - 1, own]
            return (
                (hz - hz_y) - (hy - zbackward(hy, lane)),
                (hx - zbackward(hx, lane)) - (hz - hz_x),
                (hy - hy_x) - (hx - hx_y),
            )

        def put(v, x, values):
            for c in range(3):
                fields[v, c, x, own] = values[c]
                ysend_hi[v, c, pl.ds(x - 1, 1)] = values[c][ny - 1 :]
            for slot, c in enumerate((0, 2)):
                ysend_lo[v, slot, pl.ds(x - 1, 1)] = values[c][:1]

        def update_e(h, source, v, factor, sends):
            def column(x):
                curls = curl_h(h, x)
                scale = coef[x - 1] * factor
                put(v, x, [fields[source, c, x, own] + scale * curls[c] for c in range(3)])

            def body(x, carry):
                column(x)
                return carry

            column(nx)
            column(1)
            sends(len_side)
            lax.fori_loop(2, nx, body, 0, unroll=nx - 2)
            sends(wid_side)

        def inject(n, held, v, turn_cos, turn_sin):
            for d in range(dom_len):

                def body(x, total):
                    now = [fields[n, c, x, own] for c in range(3)]
                    drive = envc[0, x - 1] * turn_cos + envc[1, x - 1] * turn_sin
                    driven = [fields[held, c, x, own] + drive * now[c] for c in range(3)]
                    dot = driven[0] * now[0] + driven[1] * now[1] + driven[2] * now[2]
                    for c in range(3):
                        fields[v, c, x, own] = driven[c]
                    return total + jnp.where(material[x - 1] == 0, dot, 0.0)

                prods[d] = lax.fori_loop(
                    1 + d * DOMLEN, 1 + (d + 1) * DOMLEN, body, jnp.zeros((ny, nz), jnp.float32), unroll=DOMLEN
                )

        def add_gradient(n):
            norm = 1.0 / math.sqrt(DOMLEN * WBLK * nz)
            at = pl.ds(n - 1, 1)
            for d in range(dom_len):
                for w in range(dom_wid):
                    block = prods[d, pl.ds(w * WBLK, WBLK)]
                    partial = jnp.sum(jnp.sum(block, axis=0, keepdims=True), axis=1, keepdims=True) * norm
                    for c in range(2):
                        term = (waves_g[c, at] * partial)[:, :bins]
                        out_g[c, d, pl.ds(w, 1)] = out_g[c, d, pl.ds(w, 1)] + term

        def envelope():
            for c in range(2):
                running = jnp.zeros((ny, nz), jnp.float32)
                for off in range(count - 1, 0, -1):
                    running = running + pre[off, c]
                for x in range(nx):
                    running = running + signs[x // DOMLEN] * (parity * waves[c][x])
                    envc[c, x] = jnp.where(material[x] == 0, running, 0.0)

        def forward(v, carry):
            @pl.when(v == 2)
            def _():
                arrive(prefix_copies())
                envelope()

            inner_h(0, v, -COURANT)

            @pl.when(v == 0)
            def _():
                arrive(first_halo())
                pl.when(has_low)(lambda: unpack_h(1))

            arrive(halo(v))
            edge_h(0, v, -COURANT)

            def sends(side):
                @pl.when(v < STEPS - 1)
                def _():
                    start(side(halo(v + 1)))

            update_e(0, v, v + 1, 1.0, sends)
            return carry

        lax.fori_loop(0, STEPS, forward, 0)

        inject(STEPS, VERSIONS, STEPS + 1, math.cos(OMEGA * STEPS), math.sin(OMEGA * STEPS))
        update_e(1, STEPS + 1, STEPS + 1, -1.0, lambda side: start(side(halo(STEPS + 1))))

        def backward(m, carry):
            v = STEPS + 1 + m
            n = STEPS - 1 - m
            inner_h(1, v, COURANT)
            add_gradient(n + 1)
            turn_cos = turn_sin = jnp.float32(0.0)
            for moment in range(1, STEPS):
                turn_cos = jnp.where(n == moment, math.cos(OMEGA * moment), turn_cos)
                turn_sin = jnp.where(n == moment, math.sin(OMEGA * moment), turn_sin)
            inject(n, v, v + 1, turn_cos, turn_sin)
            arrive(halo(v))
            edge_h(1, v, COURANT)
            update_e(1, v + 1, v + 1, -1.0, lambda side: start(side(halo(v + 1))))
            return carry

        lax.fori_loop(0, STEPS - 1, backward, 0)

        last = VERSIONS - 1
        add_gradient(1)
        for x in range(nx):
            for c in range(3):
                out_e[c, x] = fields[last, c, x + 1, own]
        inner_h(1, last, COURANT)
        arrive(halo(last))
        edge_h(1, last, COURANT)
        for x in range(nx):
            for c in range(3):
                out_h[c, x] = mags[1, c, x + 1, own]

        leave(first_halo())
        leave(prefix_copies())

        def drain(v, carry):
            @pl.when(v != STEPS)
            def _():
                leave(halo(v))

            return carry

        lax.fori_loop(0, VERSIONS, drain, 0)

    f32 = jnp.float32
    vmem = pl.BlockSpec(memory_space=pltpu.VMEM)
    hbm = pl.BlockSpec(memory_space=pl.ANY)
    smem = pl.BlockSpec(memory_space=pltpu.SMEM)
    return pl.pallas_call(
        kernel,
        out_shape=(
            jax.ShapeDtypeStruct((3, nx, ny, nz), f32),
            jax.ShapeDtypeStruct((3, nx, ny, nz), f32),
            jax.ShapeDtypeStruct((2, dom_len, dom_wid, bins), f32),
        ),
        in_specs=[hbm, hbm, hbm, hbm, hbm, smem, smem, smem],
        out_specs=(vmem, vmem, vmem),
        scratch_shapes=[
            pltpu.VMEM((VERSIONS + 1, 3, nx + 2, top + 8, nz), f32),
            pltpu.VMEM((2, 3, nx + 1, top, nz), f32),
            pltpu.VMEM((nx, ny, nz), jnp.int32),
            pltpu.VMEM((nx, ny, nz), f32),
            pltpu.VMEM((2, nx, ny, nz), f32),
            pltpu.VMEM((dom_len, ny, nz), f32),
            pltpu.VMEM((count, 2, ny, nz), f32),
            pltpu.VMEM((2, ny, nz), f32),
            pltpu.VMEM((VERSIONS, 3, nx, nz), f32),
            pltpu.VMEM((VERSIONS, 2, nx, nz), f32),
            pltpu.VMEM((VERSIONS, 3, nx, nz), f32),
            pltpu.VMEM((VERSIONS, 2, nx, nz), f32),
            pltpu.VMEM((2, 2, nx, nz), f32),
            pltpu.VMEM((2, 2, nx, nz), f32),
            pltpu.VMEM((nx + 8, nz), f32),
            pltpu.VMEM((2, STEPS, nz), f32),
            pltpu.SemaphoreType.DMA((5,)),
            pltpu.SemaphoreType.DMA((VERSIONS, 6)),
            pltpu.SemaphoreType.DMA((VERSIONS, 6)),
            pltpu.SemaphoreType.DMA((3,)),
            pltpu.SemaphoreType.DMA((3,)),
            pltpu.SemaphoreType.DMA((count,)),
            pltpu.SemaphoreType.DMA((count,)),
        ],
        compiler_params=pltpu.CompilerParams(
            collective_id=0, has_side_effects=True, vmem_limit_bytes=63 * 1024 * 1024
        ),
    )


def solution(mesh):
    count, wcount = mesh.shape["len"], mesh.shape["wid"]

    def per_device(ckpt_e, ckpt_h, adj_e, adj_h, material, inv_perm, poling, freqs):
        nx, ny, nz = material.shape
        bins = freqs.shape[0]
        call = make_kernel(count, wcount, nx, ny, nz, bins, inv_perm.shape[0])
        adjoint_e, adjoint_h, grad = call(
            ckpt_e, ckpt_h, adj_e, adj_h, material, inv_perm, poling, freqs
        )
        gradient = jnp.transpose(grad, (0, 3, 1, 2))
        return adjoint_e, adjoint_h, gradient

    field = P(None, "len", "wid", None)
    in_specs = (field, field, field, field, P("len", "wid", None), P(), P("len", "wid"), P())
    out_specs = (field, field, P(None, None, "len", "wid"))
    return jax.shard_map(
        per_device, mesh=mesh, in_specs=in_specs, out_specs=out_specs, check_vma=False
    )
```
